512 devices in a mesh: slab: 16 (over y, core), space: 32 (over z, x).
Axes of the slice: x: 4, y: 8, z: 8, core: 2. Of those that a mesh axis runs over, the one named last changes fastest.
Arguments:
- latent: bfloat16 [16, 4, 64, 32, 512], P('slab', None, 'space'), may hold values from -6.5 to 6.5
- gamma: float32 [512], replicated, may hold values from 0.25 to 1.75
- beta: float32 [512], replicated, may hold values from -3 to 3
- smooth: float32 [512], replicated, may hold values from 0.5 to 4
- weights: bfloat16 [3, 3, 3, 512, 256], P(None, None, None, 'space'), may hold values from -127 to 127, as said below
- w_scale: float32 [256], replicated, may hold values from 0.00017010345 to 0.0006804138
- bias: float32 [256], replicated, may hold values from -3 to 3
- lengths: int32 [10], replicated, may hold values from 1 to 8, 64 in all
- order: int32 [64], replicated, may hold values from 0 to 63, each once
Outputs:
- decoded: bfloat16 [16, 4, 64, 32, 256], P(None, None, 'space', 'slab')
The draws below stay inside these ranges and needn't reach their ends.
Inputs may be any that keep to these rules, and one draw needn't show every extreme that they name: `weights`: whole numbers. `order`: each frame once.
All inputs are finite; a program needn't handle non-finite values.
Results may differ from the reference program's by a relative error of at most 0.00165.
The reference program's roundings to bfloat16 on the way (of `activated`) count: a program that leaves them out, or rounds other values in their place, can miss the bound.
Values may be sent and summed in bfloat16 or wider, within the bound.
No kernel may reach another device: no remote copies, remote signals or barrier semaphores. Data moves between devices by JAX's collectives and lax.ppermute only.
A program may use at most 64 MiB of HBM per device.

```python
import math
import jax
import jax.numpy as jnp
import numpy as np
from jax import lax

C = 512
CO = 256
GROUPS = 32
FR = 4
W = 32
ROWS = 64
SLABS = 16
CLIPS = 10
MOST = 8


def draw_latent(key, part):
    key = jax.random.fold_in(key, 11)
    level_key, channel_key, drift_key, noise_key = jax.random.split(key, 4)
    group_width = C // GROUPS
    group_level = jax.random.uniform(level_key, (GROUPS,), jnp.float32, -1.5, 1.5)
    noise_part = jnp.clip(jax.random.normal(noise_key, (SLABS, FR, ROWS, W, C), jnp.float32), -4.0, 4.0)
    per_channel = jnp.repeat(group_level, group_width) + 0.4 * jax.random.uniform(channel_key, (C,), jnp.float32, -1.0, 1.0)
    slab_drift = jnp.repeat(0.6 * jax.random.uniform(drift_key, (SLABS, GROUPS), jnp.float32, -1.0, 1.0), group_width, axis=1)
    offsets = per_channel[None, :] + slab_drift
    return (noise_part + offsets[:, None, None, None, :]).astype(jnp.bfloat16)


def draw_weights(key, part):
    key = jax.random.fold_in(key, 7)
    return jax.random.randint(key, (3, 3, 3, C, CO), -127, 128).astype(jnp.bfloat16)


def split_up(number_of, total, most, slope):
    weights = [(1 << 20) // math.isqrt(standing ** slope) + 1 for standing in range(2, number_of + 1)]
    surplus, counts = total - most - (number_of - 1), [1] * (number_of - 1)
    while surplus > 0:
        movable = [i for i in range(number_of - 1) if counts[i] < most]
        whole, remaining = sum([weights[i] for i in movable]), surplus
        for i in movable:
            extra = min(most - counts[i], max(1, remaining * weights[i] // whole), surplus)
            counts[i] = counts[i] + extra
            surplus = surplus - extra
    return np.array([most] + counts)


def uneven_parts(rng, number_of, total, reach, lean):
    if number_of == 2:
        one = jax.random.randint(rng, (), max(1, total - reach), min(reach, total - 1) + 1)
        return jnp.stack([one, total - one])
    sizes = jnp.asarray(split_up(number_of, total, reach, lean), jnp.int32)
    couples = (number_of - 1) // 2
    giver, sink = sizes[1:1 + 2 * couples:2], sizes[2:2 + 2 * couples:2]
    room = jnp.minimum(giver - 1, reach - sink)
    shifted = jax.random.randint(jax.random.fold_in(rng, 1), (couples,), 0, 1 << 20) % (room + 1)
    sizes = sizes.at[1:1 + 2 * couples:2].set(giver - shifted).at[2:2 + 2 * couples:2].set(sink + shifted)
    return sizes[jax.random.permutation(jax.random.fold_in(rng, 2), number_of)]


def bell_draw(key, shape, spread, reach, kind=jnp.bfloat16):
    array = jax.random.normal(key, shape, jnp.float32) * spread
    return jnp.minimum(jnp.maximum(array, -reach), reach).astype(kind)


def setup_inputs(seed: int = 0) -> dict:
    keys = jax.random.split(jax.random.key(seed), 10)
    latent = draw_latent(jax.random.fold_in(keys[9], 71), 0)
    gamma = jnp.clip(1.0 + 0.15 * jax.random.normal(keys[1], (C,), jnp.float32), 0.25, 1.75)
    beta = bell_draw(keys[2], (C,), 0.5, 3.0, jnp.float32)
    smooth = jnp.clip(jnp.exp(jax.random.uniform(keys[3], (C,), jnp.float32, math.log(0.5), math.log(4.0))), 0.5, 4.0)
    weights = draw_weights(jax.random.fold_in(keys[9], 71), 0)
    w_scale = jnp.clip(jnp.exp(jax.random.uniform(keys[5], (CO,), jnp.float32, math.log(0.00017010345), math.log(0.0006804138))), 0.00017010345, 0.0006804138)
    bias = bell_draw(keys[6], (CO,), 0.5, 3.0, jnp.float32)
    lengths = uneven_parts(keys[7], CLIPS, FR * SLABS, MOST, 1).astype(jnp.int32)
    order = jax.random.permutation(keys[8], SLABS * FR).astype(jnp.int32)
    return {"latent": latent, "gamma": gamma, "beta": beta, "smooth": smooth, "weights": weights, "w_scale": w_scale, "bias": bias, "lengths": lengths, "order": order}


epsilon = 1e-06
highest = lax.Precision.HIGHEST

def clip_index(clip_ends, frame_ids):
    return lax.optimization_barrier(jnp.sum((clip_ends[None, :] <= frame_ids[:, None]).astype(jnp.int32), axis=1))

def reference(latent, gamma, beta, smooth, weights, w_scale, bias, lengths, order):
    all_frames = SLABS * FR
    clip_ends = jnp.cumsum(lengths).astype(jnp.int32)
    clip_starts = (clip_ends - lengths).astype(jnp.int32)
    frame_ids = jnp.arange(all_frames, dtype=jnp.int32)
    clip_ids = clip_index(clip_ends, frame_ids)
    member = clip_ids[:, None] == jnp.arange(CLIPS, dtype=jnp.int32)[None, :]
    onehot = member.astype(jnp.float32)
    frame_cells = float(ROWS * W * (C // GROUPS))
    clip_cells = jnp.dot(onehot, lengths.astype(jnp.float32), precision=highest) * frame_cells

    def clip_average(frame_sums):
        clip_sums = jnp.dot(onehot.T, frame_sums, precision=highest)
        return jnp.dot(onehot, clip_sums, precision=highest) / clip_cells[:, None]
    values = latent.astype(jnp.float32).reshape(all_frames, ROWS * W, GROUPS, C // GROUPS)
    averages = clip_average(lax.optimization_barrier(jnp.sum(values, axis=(1, 3))))
    centered = values - averages[:, None, :, None]
    variance = clip_average(lax.optimization_barrier(jnp.sum(centered * centered, axis=(1, 3))))
    inverse_std = lax.rsqrt(variance + epsilon)
    normed = (centered * inverse_std[:, None, :, None]).reshape(all_frames, ROWS, W, C) * gamma + beta
    activated = (jax.nn.silu(normed) / smooth).astype(jnp.bfloat16)
    padded = jnp.pad(activated, ((0, 0), (1, 1), (1, 1), (0, 0)))
    start_ids = lax.optimization_barrier(jnp.sum(jnp.where(member, clip_starts[None, :], 0), axis=1)).astype(jnp.int32)
    sources = jnp.maximum(frame_ids[:, None] - 2 + jnp.arange(3, dtype=jnp.int32)[None, :], start_ids[:, None])

    def one_frame(source_row):
        running = jnp.zeros((ROWS * W, CO), jnp.float32)
        for t_tap in range(3):
            frame_plane = lax.dynamic_index_in_dim(padded, source_row[t_tap], 0, keepdims=False)
            for h_tap in range(3):
                for w_tap in range(3):
                    tap_rows = frame_plane[h_tap:h_tap + ROWS, w_tap:w_tap + W].reshape(ROWS * W, C)
                    running = running + jnp.dot(tap_rows, weights[t_tap, h_tap, w_tap], preferred_element_type=jnp.float32)
        return running
    convolved = lax.map(one_frame, sources)
    decoded = (convolved * w_scale + bias).astype(jnp.bfloat16).reshape(all_frames, ROWS, W, CO)
    return jnp.take(decoded, order, axis=0).reshape(SLABS, FR, ROWS, W, CO)
```

```python
import functools
import jax
import jax.numpy as jnp
from jax import lax
from jax.experimental import pallas as pl
from jax.experimental.pallas import tpu as pltpu
from jax.sharding import Mesh, PartitionSpec as P

C = 512
CO = 256
GROUPS = 32
GW = C // GROUPS
FR = 4
W = 32
SLABS = 16
T = FR * SLABS
HALF = C // 2
NY, NC, NZ, NX = 8, 2, 8, 4
AXES = ("y", "core", "z", "x")
HIGH = lax.Precision.HIGHEST
F32 = jnp.float32
BF16 = jnp.bfloat16
CELLS = 64 * GW
FRAME_CELLS = CELLS * NZ * NX
VMEM = pl.BlockSpec(memory_space=pltpu.VMEM)
SMEM = pl.BlockSpec(memory_space=pltpu.SMEM)
ANY = pl.BlockSpec(memory_space=pl.ANY)


def iota(shape, dim):
    return lax.broadcasted_iota(jnp.int32, shape, dim)


def group_of(shape, channel_dim, group_dim):
    return (iota(shape, channel_dim) // GW == iota(shape, group_dim)).astype(F32)


def fdot(a, b):
    return jnp.dot(a, b, precision=HIGH, preferred_element_type=F32)


def bdot(a, b):
    return jnp.dot(a, b, preferred_element_type=F32)


def local_sums(x_ref, out_ref):
    rows = [x_ref[f].reshape(2 * W, C).astype(F32) for f in range(FR)]
    totals = jnp.concatenate([jnp.sum(v, axis=0, keepdims=True) for v in rows], axis=0)
    mean = fdot(totals, group_of((C, 128), 0, 1)) * (1.0 / CELLS)
    spread = fdot(mean, group_of((128, C), 1, 0))
    squares = []
    for f in range(FR):
        d = rows[f] - spread[f : f + 1]
        squares.append(jnp.sum(d * d, axis=0, keepdims=True))
    squares = fdot(jnp.concatenate(squares, axis=0), group_of((C, 128), 0, 1))
    out_ref[...] = jnp.concatenate([mean, squares], axis=0)


def join_space(in_ref, out_ref):
    v = in_ref[...]
    n = NZ * NX
    mean = jnp.sum(v[:, :FR], axis=0) * (1.0 / n)
    d = v[:, :FR] - mean[None]
    squares = jnp.sum(v[:, FR:], axis=0) + CELLS * jnp.sum(d * d, axis=0)
    out_ref[...] = jnp.concatenate([mean, squares], axis=0)


def pack(at_ref, own_ref, up_ref, down_ref, out_ref):
    z = at_ref[2]
    source = jnp.concatenate(
        [up_ref[...].reshape(FR * W, C), own_ref[...].reshape(FR * 2 * W, C), down_ref[...].reshape(FR * W, C)], axis=0
    )
    n = 4 * FR * W
    to, frm = iota((n, n), 0), iota((n, n), 1)
    col, row, frame = to // 16, (to // 4) % 4, to % 4
    want = jnp.where(
        row == 0,
        frame * W + col,
        jnp.where(row == 3, 3 * FR * W + frame * W + col, FR * W + (frame * 2 + row - 1) * W + col),
    )
    order = (want == frm).astype(F32).astype(BF16)
    roll = (iota((C, C), 0) == lax.rem(64 * z + 32 + iota((C, C), 1), C)).astype(F32).astype(BF16)
    sorted_rows = bdot(order, source).astype(BF16)
    rolled = bdot(sorted_rows, roll).astype(BF16)
    for y in range(NY):
        for core in range(NC):
            lanes = slice(HALF, C) if core == 0 else slice(0, HALF)
            lo, hi = max(4 * y - 1, 0), min(4 * y + 5, W)
            first = lo - (4 * y - 1)
            out_ref[2 * y + core, 16 * first : 16 * (first + hi - lo), :] = rolled[16 * lo : 16 * hi, lanes]
            if y == 0:
                out_ref[2 * y + core, 0:16, :] = jnp.zeros((16, HALF), BF16)
            if y == NY - 1:
                out_ref[2 * y + core, 80:96, :] = jnp.zeros((16, HALF), BF16)


def starts(lengths_ref, frame):
    end = lengths_ref[0]
    start = jnp.zeros_like(frame)
    for k in range(1, lengths_ref.shape[0]):
        start = jnp.where(frame >= end, end, start)
        end = end + lengths_ref[k]
    return start


def convolve(
    at_ref, lengths_ref, sums_ref, gamma_ref, beta_ref, smooth_ref, x_ref, own, r1, r2, r3, r4,
    keep_ref, send_ref, w_ref, act_ref, acc_ref, sem,
):
    y, core, z, s = at_ref[0], at_ref[1], at_ref[2], at_ref[3]
    copies = []

    def bring(source, count, first, row):
        for i in range(count):
            at = pl.multiple_of(row + 16 * i, 16)
            copy = pltpu.make_async_copy(
                source.at[first + i], w_ref.at[:, pl.ds(at, 16), :], sem.at[len(copies)]
            )
            copy.start()
            copies.append(copy)

    bring(own, 2, 2 * core, jnp.where(core == 0, 224, 0))
    bring(r1, 4, 0, jnp.where(core == 0, 160, 32))
    bring(r2, 4, 0, 96)
    bring(r3, 4, 0, jnp.where(core == 0, 32, 160))
    bring(r4, 2, 0, jnp.where(core == 0, 0, 224))

    n = 2 * T
    sums = sums_ref[...].reshape(n, 128)
    frame_a = (iota((n, n), 0) // 8) * FR + iota((n, n), 0) % FR
    frame_b = (iota((n, n), 1) // 8) * FR + iota((n, n), 1) % FR
    squares_b = (iota((n, n), 1) // 4) % 2
    same = starts(lengths_ref, frame_a) == starts(lengths_ref, frame_b)
    on_means = (same & (squares_b == 0)).astype(F32)
    on_squares = (same & (squares_b == 1)).astype(F32)
    count = jnp.sum(on_means, axis=1, keepdims=True)
    mean = fdot(on_means, sums) / count
    off = sums - mean
    variance = (fdot(on_squares, sums) + FRAME_CELLS * fdot(on_means, off * off)) / (count * FRAME_CELLS)
    inverse = lax.rsqrt(variance + 1e-6)
    pick = (
        (iota((T, n), 1) // 8 * FR + iota((T, n), 1) % FR == iota((T, n), 0)) & ((iota((T, n), 1) // 4) % 2 == 0)
    ).astype(F32)
    base = 64 * z + jnp.where(core == 0, 32 + HALF, 32)
    mine = (iota((C, HALF), 0) == lax.rem(base + iota((C, HALF), 1), C)).astype(F32)
    to_group = (iota((128, HALF), 0) == lax.rem(base + iota((128, HALF), 1), C) // GW).astype(F32)
    gamma, beta, smooth = fdot(gamma_ref[...], mine), fdot(beta_ref[...], mine), fdot(smooth_ref[...], mine)
    mean = fdot(fdot(pick, mean), to_group)
    scale = fdot(fdot(pick, inverse), to_group) * gamma
    unsmooth = 1.0 / smooth

    m = 16 * 16
    to, frm = iota((m, m), 0), iota((m, m), 1)
    row, t = to // T, to % T
    by_row = (frm == (t // FR) * 16 + row * FR + t % FR).astype(F32).astype(BF16)
    frame, other = iota((T, T), 0), iota((T, T), 1)
    start = starts(lengths_ref, frame)
    before = jnp.maximum(frame - 1, start)
    before2 = jnp.maximum(frame - 2, start)
    earlier = jnp.concatenate([(other == before2).astype(F32), (other == before).astype(F32)], axis=0).astype(BF16)
    for c in range(6):
        rows = x_ref[:, 16 * c : 16 * (c + 1), :].reshape(m, HALF)
        values = bdot(by_row, rows)
        for r in range(4):
            v = (values[T * r : T * (r + 1)] - mean) * scale + beta
            v = v / (1.0 + jnp.exp(-v)) * unsmooth
            inside = None
            if r == 0:
                inside = s > 0
            if r == 3:
                inside = s < NZ * NX - 1
            if c == 0:
                inside = (y > 0) if inside is None else inside & (y > 0)
            if c == 5:
                inside = (y < NY - 1) if inside is None else inside & (y < NY - 1)
            if inside is not None:
                v = v * inside.astype(F32)
            v = v.astype(BF16)
            act_ref[2, r, c] = v
            e = bdot(earlier, v).astype(BF16)
            act_ref[0, r, c] = e[:T]
            act_ref[1, r, c] = e[T:]

    for copy in copies:
        copy.wait()
    total = None
    for j in range(3):
        for a in range(3):
            for b in range(3):
                lhs = act_ref[j, a : a + 2, b : b + 4].reshape(8 * T, HALF)
                term = bdot(lhs, w_ref[9 * j + 3 * a + b])
                total = term if total is None else total + term
    acc_ref[...] = total.reshape(2, 4, T, CO)
    keep_ref[...] = acc_ref[:, pl.ds(2 * core, 2)]
    send_ref[...] = acc_ref[:, pl.ds(2 - 2 * core, 2)]


def finish(order_ref, scale_ref, bias_ref, a_ref, b_ref, out_ref):
    picked = (iota((T, T), 0) == order_ref[...]).astype(F32).astype(BF16)
    for r in range(2):
        for c in range(2):
            v = ((a_ref[r, c] + b_ref[r, c]) * scale_ref[...] + bias_ref[...]).astype(BF16)
            v = lax.dot_general(picked, v, (((0,), (0,)), ((), ())), preferred_element_type=F32)
            at = (2 * r + c) * CO
            out_ref[:, at : at + CO] = v.astype(BF16)


def shift(value, step):
    pairs = []
    for i in range(NY * NC * NZ * NX):
        y, core, z, x = i // 64, i // 32 % 2, i // 4 % 8, i % 4
        to = step(y, core, z, x)
        if to is not None:
            ty, tc, tz, tx = to
            pairs.append((i, ((ty * NC + tc) * NZ + tz % NZ) * NX + tx))
    return lax.ppermute(value, AXES, pairs)


def by_space(y, core, s):
    return (y, core, s // NX, s % NX) if 0 <= s < NZ * NX else None


def struct(shape, dtype):
    return jax.ShapeDtypeStruct(shape, dtype)


def params(mib=48):
    return pltpu.CompilerParams(vmem_limit_bytes=mib * 2**20)


def cost(flops, size):
    return pl.CostEstimate(flops=flops, bytes_accessed=size, transcendentals=0)


def local(latent, gamma, beta, smooth, weights, w_scale, bias, lengths, order):
    y, core, z, x = (lax.axis_index(a) for a in AXES)
    at = jnp.stack([y, core, z, z * NX + x]).astype(jnp.int32)
    latent = latent[0]
    weights = weights.reshape(27, GW, CO)

    own = lax.all_to_all(jnp.broadcast_to(weights[None], (NX, 27, GW, CO)), "x", 0, 0, tiled=True)

    sums = pl.pallas_call(
        local_sums, out_shape=struct((8, 128), F32), in_specs=[VMEM], out_specs=VMEM, compiler_params=params(),
        cost_estimate=cost(2**20, 2**18),
    )(latent)
    up = shift(latent[:, 1], lambda y, core, z, x: by_space(y, core, z * NX + x + 1))
    down = shift(latent[:, 0], lambda y, core, z, x: by_space(y, core, z * NX + x - 1))
    gathered = lax.all_to_all(jnp.broadcast_to(sums[None], (NZ * NX, 8, 128)), ("z", "x"), 0, 0, tiled=True)

    def ring(v):
        return shift(v, lambda y, core, z, x: (y, core, z + 1 - 2 * core, x))

    r1 = ring(own)
    windows = pl.pallas_call(
        pack, out_shape=struct((SLABS, 96, HALF), BF16), in_specs=[SMEM, VMEM, VMEM, VMEM], out_specs=VMEM,
        compiler_params=params(), cost_estimate=cost(2**29, 2**21),
    )(at, latent, up, down)
    columns = lax.all_to_all(windows, ("y", "core"), 0, 0, tiled=True)
    sums = pl.pallas_call(
        join_space, out_shape=struct((8, 128), F32), in_specs=[VMEM], out_specs=VMEM, compiler_params=params(),
        cost_estimate=cost(2**18, 2**17),
    )(gathered)
    sums = lax.all_to_all(jnp.broadcast_to(sums[None], (SLABS, 8, 128)), ("y", "core"), 0, 0, tiled=True)
    r2 = ring(r1)
    r3 = ring(r2)
    r4 = ring(jnp.where(core == 0, r3[2:], r3[:2]))

    part = struct((2, 2, T, CO), F32)
    keep, send = pl.pallas_call(
        convolve, out_shape=(part, part), in_specs=[SMEM, SMEM] + [VMEM] * 5 + [ANY] * 5, out_specs=(VMEM, VMEM),
        scratch_shapes=[
            pltpu.VMEM((27, HALF, CO), BF16),
            pltpu.VMEM((3, 4, 6, T, HALF), BF16),
            pltpu.VMEM((2, 4, T, CO), F32),
            pltpu.SemaphoreType.DMA((16,)),
        ],
        compiler_params=params(), cost_estimate=cost(2**31, 2**22),
    )(at, lengths, sums, gamma[None], beta[None], smooth[None], columns, own, r1, r2, r3, r4)
    other = shift(send, lambda y, core, z, x: (y, 1 - core, z, x))
    out = pl.pallas_call(
        finish, out_shape=struct((T, 4 * CO), BF16), in_specs=[VMEM] * 5, out_specs=VMEM, compiler_params=params(),
        cost_estimate=cost(2**22, 2**20),
    )(order[None], w_scale[None], bias[None], keep, other)
    return out.reshape(SLABS, FR, 2, 2, CO)


def solution(mesh):
    inner = Mesh(mesh.devices.reshape(NY, NC, NZ, NX), AXES)
    slab, space = ("y", "core"), ("z", "x")
    in_specs = (
        P(slab, None, space, None, None), P(), P(), P(), P(None, None, None, space, None), P(), P(), P(), P(),
    )
    out_specs = P(None, None, space, slab, None)
    return jax.shard_map(local, mesh=inner, in_specs=in_specs, out_specs=out_specs, check_vma=False)
```

```python
import functools
import jax
import jax.numpy as jnp
from jax import lax
from jax.experimental import pallas as pl
from jax.experimental.pallas import tpu as pltpu
from jax.sharding import Mesh, PartitionSpec as P

C = 512
CO = 256
GROUPS = 32
GW = C // GROUPS
FR = 4
W = 32
SLABS = 16
T = FR * SLABS
HALF = C // 2
NY, NC, NZ, NX = 8, 2, 8, 4
AXES = ("y", "core", "z", "x")
HIGH = lax.Precision.HIGHEST
F32 = jnp.float32
BF16 = jnp.bfloat16
CELLS = 64 * GW
FRAME_CELLS = CELLS * NZ * NX
VMEM = pl.BlockSpec(memory_space=pltpu.VMEM)
SMEM = pl.BlockSpec(memory_space=pltpu.SMEM)
ANY = pl.BlockSpec(memory_space=pl.ANY)


def iota(shape, dim):
    return lax.broadcasted_iota(jnp.int32, shape, dim)


def group_of(shape, channel_dim, group_dim):
    return (iota(shape, channel_dim) // GW == iota(shape, group_dim)).astype(F32)


def fdot(a, b):
    return jnp.dot(a, b, precision=HIGH, preferred_element_type=F32)


def bdot(a, b):
    return jnp.dot(a, b, preferred_element_type=F32)


def local_sums(x_hbm, sums_ref, x_ref, sem):
    loads = [pltpu.make_async_copy(x_hbm.at[f], x_ref.at[f], sem.at[f]) for f in range(FR)]
    for copy in loads:
        copy.start()
    rows = []
    for f in range(FR):
        loads[f].wait()
        rows.append(x_ref[f].reshape(2 * W, C).astype(F32))
    totals = jnp.concatenate([jnp.sum(v, axis=0, keepdims=True) for v in rows], axis=0)
    mean = fdot(totals, group_of((C, 128), 0, 1)) * (1.0 / CELLS)
    spread = fdot(mean, group_of((128, C), 1, 0))
    squares = []
    for f in range(FR):
        d = rows[f] - spread[f : f + 1]
        squares.append(jnp.sum(d * d, axis=0, keepdims=True))
    squares = fdot(jnp.concatenate(squares, axis=0), group_of((C, 128), 0, 1))
    sums_ref[...] = jnp.broadcast_to(jnp.concatenate([mean, squares], axis=0)[None], sums_ref.shape)


def join_space(v):
    n = NZ * NX
    mean = jnp.sum(v[:, :FR], axis=0) * (1.0 / n)
    d = v[:, :FR] - mean[None]
    squares = jnp.sum(v[:, FR:], axis=0) + CELLS * jnp.sum(d * d, axis=0)
    return jnp.concatenate([mean, squares], axis=0)


def in_three(v):
    high = v.astype(BF16)
    rest = v - high.astype(F32)
    middle = rest.astype(BF16)
    return high, middle, (rest - middle.astype(F32)).astype(BF16)


def channel_at(z, x, place):
    u = place + 32
    block, shard = lax.rem(z + u // (GW * NX), NZ), lax.rem(x + u // GW, NX)
    return block * (GW * NX) + shard * GW + u % GW


def pack(at_ref, own_ref, up_ref, down_ref, sums_ref, out_ref):
    z, x = at_ref[2], at_ref[4]
    source = jnp.concatenate(
        [up_ref[...].reshape(FR * W, C), own_ref[...].reshape(FR * 2 * W, C), down_ref[...].reshape(FR * W, C)], axis=0
    )
    n = 4 * FR * W
    to, frm = iota((n, n), 0), iota((n, n), 1)
    col, row, frame = to // 16, (to // 4) % 4, to % 4
    want = jnp.where(
        row == 0,
        frame * W + col,
        jnp.where(row == 3, 3 * FR * W + frame * W + col, FR * W + (frame * 2 + row - 1) * W + col),
    )
    order = (want == frm).astype(F32).astype(BF16)
    roll = (iota((C, C), 0) == channel_at(z, x, iota((C, C), 1))).astype(F32).astype(BF16)
    sorted_rows = bdot(order, source).astype(BF16)
    rolled = bdot(sorted_rows, roll).astype(BF16)
    sums = jnp.concatenate([join_space(sums_ref[...]), jnp.zeros((8, 128), F32)], axis=0)
    high, middle, low = in_three(sums)
    thirds = jnp.concatenate([high[:, :GROUPS], middle[:, :GROUPS], low[:, :GROUPS]], axis=1)
    thirds = jnp.concatenate([thirds, jnp.zeros((16, HALF - 3 * GROUPS), BF16)], axis=1)
    for y in range(NY):
        for core in range(NC):
            lanes = slice(HALF, C) if core == 0 else slice(0, HALF)
            lo, hi = max(4 * y - 1, 0), min(4 * y + 5, W)
            first = lo - (4 * y - 1)
            out_ref[2 * y + core, 16 * first : 16 * (first + hi - lo), :] = rolled[16 * lo : 16 * hi, lanes]
            out_ref[2 * y + core, 96:112, :] = thirds
            if y == 0:
                out_ref[2 * y + core, 0:16, :] = jnp.zeros((16, HALF), BF16)
            if y == NY - 1:
                out_ref[2 * y + core, 80:96, :] = jnp.zeros((16, HALF), BF16)


def starts(lengths_ref, frame):
    end = lengths_ref[0]
    start = jnp.zeros_like(frame)
    for k in range(1, lengths_ref.shape[0]):
        start = jnp.where(frame >= end, end, start)
        end = end + lengths_ref[k]
    return start


def activate(at_ref, lengths_ref, gamma_ref, beta_ref, smooth_ref, x_ref, act_ref):
    y, core, z, s, x = at_ref[0], at_ref[1], at_ref[2], at_ref[3], at_ref[4]
    n = 2 * T
    thirds = x_ref[:, 96:112, :].astype(F32)[:, :8, :128].reshape(n, 128)
    add = ((iota((128, 128), 0) % GROUPS == iota((128, 128), 1)) & (iota((128, 128), 0) < 3 * GROUPS)).astype(F32)
    sums = fdot(thirds, add)
    frame_a = (iota((n, n), 0) // 8) * FR + iota((n, n), 0) % FR
    frame_b = (iota((n, n), 1) // 8) * FR + iota((n, n), 1) % FR
    squares_b = (iota((n, n), 1) // 4) % 2
    same = starts(lengths_ref, frame_a) == starts(lengths_ref, frame_b)
    on_means = (same & (squares_b == 0)).astype(F32)
    on_squares = (same & (squares_b == 1)).astype(F32)
    count = jnp.sum(on_means, axis=1, keepdims=True)
    mean = fdot(on_means, sums) / count
    off = sums - mean
    variance = (fdot(on_squares, sums) + FRAME_CELLS * fdot(on_means, off * off)) / (count * FRAME_CELLS)
    inverse = lax.rsqrt(variance + 1e-6)
    pick = (
        (iota((T, n), 1) // 8 * FR + iota((T, n), 1) % FR == iota((T, n), 0)) & ((iota((T, n), 1) // 4) % 2 == 0)
    ).astype(F32)
    first = jnp.where(core == 0, HALF, 0)
    mine = (iota((C, HALF), 0) == channel_at(z, x, first + iota((C, HALF), 1))).astype(F32)
    to_group = (iota((128, HALF), 0) == channel_at(z, x, first + iota((128, HALF), 1)) // GW).astype(F32)
    gamma, beta, smooth = fdot(gamma_ref[...], mine), fdot(beta_ref[...], mine), fdot(smooth_ref[...], mine)
    mean = fdot(fdot(pick, mean), to_group)
    scale = fdot(fdot(pick, inverse), to_group) * gamma
    unsmooth = 1.0 / smooth

    m = 16 * 16
    to, frm = iota((m, m), 0), iota((m, m), 1)
    row, t = to // T, to % T
    by_row = (frm == (t // FR) * 16 + row * FR + t % FR).astype(F32).astype(BF16)
    frame, other = iota((T, T), 0), iota((T, T), 1)
    start = starts(lengths_ref, frame)
    before = jnp.maximum(frame - 1, start)
    before2 = jnp.maximum(frame - 2, start)
    earlier = jnp.concatenate([(other == before2).astype(F32), (other == before).astype(F32)], axis=0).astype(BF16)
    for c in range(6):
        rows = x_ref[:, 16 * c : 16 * (c + 1), :].reshape(m, HALF)
        values = bdot(by_row, rows)
        for r in range(4):
            v = (values[T * r : T * (r + 1)] - mean) * scale + beta
            v = v / (1.0 + jnp.exp(-v)) * unsmooth
            inside = None
            if r == 0:
                inside = s > 0
            if r == 3:
                inside = s < NZ * NX - 1
            if c == 0:
                inside = (y > 0) if inside is None else inside & (y > 0)
            if c == 5:
                inside = (y < NY - 1) if inside is None else inside & (y < NY - 1)
            if inside is not None:
                v = v * inside.astype(F32)
            v = v.astype(BF16)
            act_ref[2, r, c] = v
            e = bdot(earlier, v).astype(BF16)
            act_ref[0, r, c] = e[:T]
            act_ref[1, r, c] = e[T:]


def convolve(at_ref, act_hbm, a0, b0, a1, b1, a2, b2, a3, b3, r4, keep_ref, send_ref, w_ref, act_ref, acc_ref, sem, act_sem):
    core = at_ref[1]
    copies = []

    def bring(source, count, first, row):
        for i in range(count):
            at = pl.multiple_of(row + 16 * i, 16)
            copy = pltpu.make_async_copy(source.at[first + i], w_ref.at[:, pl.ds(at, 16), :], sem.at[len(copies)])
            copy.start()
            copies.append(copy)

    moves = [pltpu.make_async_copy(act_hbm.at[j], act_ref.at[j], act_sem.at[j]) for j in range(3)]
    for move in moves:
        move.start()
    own_sems = [sem.at[0], sem.at[1]]

    @pl.when(core == 0)
    def _():
        for i in range(2):
            pltpu.make_async_copy(a0.at[i], w_ref.at[:, pl.ds(224 + 16 * i, 16), :], own_sems[i]).start()

    @pl.when(core == 1)
    def _():
        for i in range(2):
            pltpu.make_async_copy(b0.at[i], w_ref.at[:, pl.ds(16 * i, 16), :], own_sems[i]).start()

    copies += [pltpu.make_async_copy(a0.at[i], w_ref.at[:, pl.ds(16 * i, 16), :], own_sems[i]) for i in range(2)]
    bring(a1, 2, 0, jnp.where(core == 0, 160, 32))
    bring(b1, 2, 0, jnp.where(core == 0, 192, 64))
    bring(a2, 2, 0, 96)
    bring(b2, 2, 0, 128)
    bring(a3, 2, 0, jnp.where(core == 0, 32, 160))
    bring(b3, 2, 0, jnp.where(core == 0, 64, 192))
    bring(r4, 2, 0, jnp.where(core == 0, 0, 224))

    for copy in copies:
        copy.wait()
    total = None
    for tap in range(27):
        j, a, b = tap // 9, tap // 3 % 3, tap % 3
        if tap % 9 == 0:
            moves[j].wait()
        lhs = act_ref[j, a : a + 2, b : b + 4].reshape(8 * T, HALF)
        term = bdot(lhs, w_ref[tap])
        total = term if total is None else total + term
    acc_ref[...] = total.reshape(2, 4, T, CO)
    keep_ref[...] = acc_ref[:, pl.ds(2 * core, 2)]
    send_ref[...] = acc_ref[:, pl.ds(2 - 2 * core, 2)]


def finish(order_ref, scale_ref, bias_ref, a_ref, b_ref, out_ref):
    picked = (iota((T, T), 0) == order_ref[...]).astype(F32).astype(BF16)
    for r in range(2):
        for c in range(2):
            v = ((a_ref[r, c] + b_ref[r, c]) * scale_ref[...] + bias_ref[...]).astype(BF16)
            v = lax.dot_general(picked, v, (((0,), (0,)), ((), ())), preferred_element_type=F32)
            at = (2 * r + c) * CO
            out_ref[:, at : at + CO] = v.astype(BF16)


def shift(value, step):
    pairs = []
    for i in range(NY * NC * NZ * NX):
        y, core, z, x = i // 64, i // 32 % 2, i // 4 % 8, i % 4
        to = step(y, core, z, x)
        if to is not None:
            ty, tc, tz, tx = to
            pairs.append((i, ((ty * NC + tc) * NZ + tz % NZ) * NX + tx))
    return lax.ppermute(value, AXES, pairs)


def by_space(y, core, s):
    return (y, core, s // NX, s % NX) if 0 <= s < NZ * NX else None


def struct(shape, dtype):
    return jax.ShapeDtypeStruct(shape, dtype)


def params(mib=48):
    return pltpu.CompilerParams(vmem_limit_bytes=mib * 2**20)


def cost(flops, size):
    return pl.CostEstimate(flops=flops, bytes_accessed=size, transcendentals=0)


def local(latent, gamma, beta, smooth, weights, w_scale, bias, lengths, order):
    y, core, z, x = (lax.axis_index(a) for a in AXES)
    at = jnp.stack([y, core, z, z * NX + x, x]).astype(jnp.int32)
    latent = latent[0]
    weights = weights.reshape(27, GW, CO)

    spread = pl.pallas_call(
        local_sums, out_shape=struct((NZ * NX, 8, 128), F32), in_specs=[ANY], out_specs=VMEM,
        scratch_shapes=[pltpu.VMEM((FR, 2, W, C), BF16), pltpu.SemaphoreType.DMA((FR,))],
        compiler_params=params(60), cost_estimate=cost(2**16, 2**16),
    )(latent)

    def ring(v):
        return shift(v, lambda y, core, z, x: (y, core, z + 1 - 2 * core, x))

    def beside(d):
        return shift(weights, lambda y, core, z, x: (y, core, z, (x - d) % NX))

    x1, x2, x3 = beside(1), beside(2), beside(3)
    up = shift(latent[:, 1], lambda y, core, z, x: by_space(y, core, z * NX + x + 1))
    down = shift(latent[:, 0], lambda y, core, z, x: by_space(y, core, z * NX + x - 1))
    gathered = lax.all_to_all(spread, ("z", "x"), 0, 0, tiled=True)
    a0, b0 = jnp.stack([weights, x1]), jnp.stack([x2, x3])
    gathered, a0, b0, up, down = lax.optimization_barrier((gathered, a0, b0, up, down))
    a1, b1 = ring(a0), ring(b0)
    windows = pl.pallas_call(
        pack, out_shape=struct((SLABS, 112, HALF), BF16), in_specs=[SMEM] + [VMEM] * 4, out_specs=VMEM,
        compiler_params=params(), cost_estimate=cost(2**16, 2**16),
    )(at, latent, up, down, gathered)
    columns = lax.all_to_all(windows, ("y", "core"), 0, 0, tiled=True)
    a2, b2 = ring(a1), ring(b1)
    a3, b3 = ring(a2), ring(b2)
    act = pl.pallas_call(
        activate, out_shape=struct((3, 4, 6, T, HALF), BF16), in_specs=[SMEM, SMEM] + [VMEM] * 4, out_specs=VMEM,
        compiler_params=params(), cost_estimate=cost(2**16, 2**16),
    )(at, lengths, gamma[None], beta[None], smooth[None], columns)
    r4 = ring(jnp.where(core == 0, b3, a3))

    part = struct((2, 2, T, CO), F32)
    keep, send = pl.pallas_call(
        convolve, out_shape=(part, part), in_specs=[SMEM] + [ANY] * 10, out_specs=(VMEM, VMEM),
        scratch_shapes=[
            pltpu.VMEM((27, HALF, CO), BF16),
            pltpu.VMEM((3, 4, 6, T, HALF), BF16),
            pltpu.VMEM((2, 4, T, CO), F32),
            pltpu.SemaphoreType.DMA((16,)),
            pltpu.SemaphoreType.DMA((3,)),
        ],
        compiler_params=params(60), cost_estimate=cost(2**16, 2**16),
    )(at, act, a0, b0, a1, b1, a2, b2, a3, b3, r4)
    other = shift(send, lambda y, core, z, x: (y, 1 - core, z, x))
    out = pl.pallas_call(
        finish, out_shape=struct((T, 4 * CO), BF16), in_specs=[VMEM] * 5, out_specs=VMEM, compiler_params=params(),
        cost_estimate=cost(2**22, 2**20),
    )(order[None], w_scale[None], bias[None], keep, other)
    return out.reshape(SLABS, FR, 2, 2, CO)


def solution(mesh):
    inner = Mesh(mesh.devices.reshape(NY, NC, NZ, NX), AXES)
    slab, space = ("y", "core"), ("z", "x")
    in_specs = (
        P(slab, None, space, None, None), P(), P(), P(), P(None, None, None, space, None), P(), P(), P(), P(),
    )
    out_specs = P(None, None, space, slab, None)
    return jax.shard_map(local, mesh=inner, in_specs=in_specs, out_specs=out_specs, check_vma=False)
```

```python
import functools
import jax
import jax.numpy as jnp
from jax import lax
from jax.experimental import pallas as pl
from jax.experimental.pallas import tpu as pltpu
from jax.sharding import Mesh, PartitionSpec as P

C = 512
CO = 256
GROUPS = 32
GW = C // GROUPS
FR = 4
W = 32
SLABS = 16
T = FR * SLABS
HALF = C // 2
SHARD = 27 * GW
EDGE = FR * W
NY, NC, NZ, NX = 8, 2, 8, 4
AXES = ("y", "core", "z", "x")
HIGH = lax.Precision.HIGHEST
F32 = jnp.float32
BF16 = jnp.bfloat16
CELLS = 64 * GW
FRAME_CELLS = CELLS * NZ * NX
VMEM = pl.BlockSpec(memory_space=pltpu.VMEM)
SMEM = pl.BlockSpec(memory_space=pltpu.SMEM)
ANY = pl.BlockSpec(memory_space=pl.ANY)


def iota(shape, dim):
    return lax.broadcasted_iota(jnp.int32, shape, dim)


def group_of(shape, channel_dim, group_dim):
    return flag((iota(shape, channel_dim) >> 4) == iota(shape, group_dim))


def flag(condition):
    return condition.astype(F32).astype(BF16)


def bdot(a, b):
    return jnp.dot(a, b, preferred_element_type=F32)


def in_three(v):
    high = v.astype(BF16)
    rest = v - high.astype(F32)
    middle = rest.astype(BF16)
    return high, middle, (rest - middle.astype(F32)).astype(BF16)


def take(v, picks):
    n = v.shape[0]
    pad = -n % 8
    parts = [jnp.concatenate([p.astype(F32), jnp.zeros((pad, v.shape[1]), F32)], axis=0) for p in in_three(v)]
    out = bdot(jnp.concatenate(parts, axis=0).astype(BF16), picks)
    return out[:n] + out[n + pad : 2 * n + pad] + out[2 * (n + pad) : 3 * n + 2 * pad]


def prepare(x_hbm, w_ref, sums_ref, next_ref, prev_ref, x_ref, sem):
    loads = [pltpu.make_async_copy(x_hbm.at[f], x_ref.at[f], sem.at[f]) for f in range(FR)]
    for copy in loads:
        copy.start()
    for out_ref in (next_ref, prev_ref):
        out_ref[:SHARD] = w_ref[...].reshape(SHARD, CO)
    to_groups, to_channels = group_of((C, 128), 0, 1), group_of((128, C), 1, 0)
    rows = []
    for f in range(FR):
        loads[f].wait()
        rows.append(x_ref[f].reshape(2 * W, C).astype(F32))
    totals = jnp.concatenate([jnp.sum(v, axis=0, keepdims=True) for v in rows], axis=0)
    mean = take(totals, to_groups) * (1.0 / CELLS)
    spread = take(mean, to_channels)
    squares = []
    for f in range(FR):
        d = rows[f] - spread[f : f + 1]
        squares.append(jnp.sum(d * d, axis=0, keepdims=True))
    squares = take(jnp.concatenate(squares, axis=0), to_groups)
    for out_ref, row in ((next_ref, 1), (prev_ref, 0)):
        edge = x_ref[:, row].reshape(EDGE, C)
        out_ref[SHARD : SHARD + EDGE] = edge[:, :HALF]
        out_ref[SHARD + EDGE :] = edge[:, HALF:]
    sums_ref[...] = jnp.broadcast_to(jnp.concatenate([mean, squares], axis=0)[None], sums_ref.shape)


def join_space(v):
    n = NZ * NX
    mean = jnp.sum(v[:, :FR], axis=0) * (1.0 / n)
    d = v[:, :FR] - mean[None]
    squares = jnp.sum(v[:, FR:], axis=0) + CELLS * jnp.sum(d * d, axis=0)
    return jnp.concatenate([mean, squares], axis=0)


def channel_at(s, core, place):
    step = (place + 2 * GW) >> 6
    nth = jnp.where(step == 0, place >> 4, ((place >> 4) + 2) & 3)
    away = jnp.where(core == 0, jnp.where(nth == 2, -1, jnp.where(nth == 3, 2, nth)), jnp.where(nth == 0, 2, nth - 2))
    away = away + NX * jnp.where(core == 0, -step, step)
    return (((s + away) & (NZ * NX - 1)) << 4) + (place & 15)


def pack(at_ref, own_ref, up_ref, down0_ref, down1_ref, sums_ref, out_ref):
    s = at_ref[2]

    def edge(ref):
        return jnp.concatenate([ref[SHARD : SHARD + EDGE], ref[SHARD + EDGE :]], axis=1)

    down = jnp.where(at_ref[1] == 0, edge(down0_ref), edge(down1_ref))
    source = jnp.concatenate([edge(up_ref), own_ref[...].reshape(2 * EDGE, C), down], axis=0)
    n = 4 * FR * W
    to = iota((n, 1), 0)
    col, row, frame = to >> 4, (to >> 2) & 3, to & 3
    want = jnp.where(
        row == 0,
        frame * W + col,
        jnp.where(row == 3, 3 * EDGE + frame * W + col, EDGE + (frame * 2 + row - 1) * W + col),
    )
    order = flag(want == iota((n, n), 1))
    place = iota((1, C), 1)
    roll = flag(iota((C, C), 0) == channel_at(s, place >> 8, place & (HALF - 1)))
    sorted_rows = bdot(order, source).astype(BF16)
    rolled = bdot(sorted_rows, roll).astype(BF16)
    sums = jnp.concatenate([join_space(sums_ref[...]), jnp.zeros((8, 128), F32)], axis=0)
    thirds = [p[:, :GROUPS] for p in in_three(sums)]
    thirds = jnp.concatenate(thirds + [jnp.zeros((16, HALF - 3 * GROUPS), BF16)], axis=1)
    for y in range(NY):
        for core in range(NC):
            lanes = slice(HALF * core, HALF * (core + 1))
            lo, hi = max(4 * y - 1, 0), min(4 * y + 5, W)
            first = lo - (4 * y - 1)
            out_ref[2 * y + core, 16 * first : 16 * (first + hi - lo), :] = rolled[16 * lo : 16 * hi, lanes]
            out_ref[2 * y + core, 96:112, :] = thirds
            if y == 0:
                out_ref[2 * y + core, 0:16, :] = jnp.zeros((16, HALF), BF16)
            if y == NY - 1:
                out_ref[2 * y + core, 80:96, :] = jnp.zeros((16, HALF), BF16)


def starts(lengths_ref, frame):
    end = lengths_ref[0]
    start = jnp.zeros_like(frame)
    for k in range(1, lengths_ref.shape[0]):
        start = jnp.where(frame >= end, end, start)
        end = end + lengths_ref[k]
    return start


def activate(at_ref, lengths_ref, gamma_ref, beta_ref, smooth_ref, x_ref, act_ref):
    y, core, s = at_ref[0], at_ref[1], at_ref[2]
    n = 2 * T
    thirds = x_ref[:, 96:112, :].astype(F32)[:, :8, :128].reshape(n, 128)
    rows, columns = iota((n, 1), 0), iota((1, n), 1)
    frame_a, frame_b = (rows >> 3) * FR + (rows & 3), (columns >> 3) * FR + (columns & 3)
    same = starts(lengths_ref, frame_a) == starts(lengths_ref, frame_b)
    means_b = (columns & 4) == 0
    on_means, on_squares = same & means_b, flag(same & jnp.logical_not(means_b))
    count = jnp.sum(on_means.astype(F32), axis=1, keepdims=True)
    on_means = flag(on_means)

    def whole(v):
        return v[:, :GROUPS] + v[:, GROUPS : 2 * GROUPS] + v[:, 2 * GROUPS : 3 * GROUPS]

    def parts(v):
        return jnp.concatenate(list(in_three(v)) + [jnp.zeros((n, 128 - 3 * GROUPS), BF16)], axis=1)

    mean = whole(bdot(on_means, thirds.astype(BF16))) / count
    off = whole(thirds) - mean
    squares = whole(bdot(on_squares, thirds.astype(BF16))) + FRAME_CELLS * whole(bdot(on_means, parts(off * off)))
    inverse = lax.rsqrt(squares / (count * FRAME_CELLS) + 1e-6)
    pick = flag((frame_b == iota((T, 1), 0)) & means_b)
    channels = channel_at(s, core, iota((1, HALF), 1))
    mine = flag(iota((C, HALF), 0) == channels)
    third = iota((128, 1), 0)
    to_group = flag(((third & (GROUPS - 1)) == (channels >> 4)) & (third < 3 * GROUPS))
    affine = take(jnp.concatenate([gamma_ref[...], beta_ref[...], smooth_ref[...]], axis=0), mine)
    gamma, beta, unsmooth = affine[0:1], affine[1:2], 1.0 / affine[2:3]
    mean = bdot(bdot(pick, parts(mean)).astype(BF16), to_group)
    scale = bdot(bdot(pick, parts(inverse)).astype(BF16), to_group) * gamma

    m = 16 * 16
    to = iota((m, 1), 0)
    row, t = to >> 6, to & (T - 1)
    by_row = flag(iota((m, m), 1) == (t >> 2) * 16 + row * FR + (t & 3))
    frame, other = iota((T, 1), 0), iota((T, T), 1)
    start = starts(lengths_ref, frame)
    earlier = [flag(other == jnp.maximum(frame - back, start)) for back in (2, 1)]
    earlier = jnp.concatenate(earlier, axis=0)
    for c in range(6):
        rows = x_ref[:, 16 * c : 16 * (c + 1), :].reshape(m, HALF)
        values = bdot(by_row, rows)
        for r in range(4):
            v = (values[T * r : T * (r + 1)] - mean) * scale + beta
            v = v / (1.0 + jnp.exp(-v)) * unsmooth
            inside = None
            if r == 0:
                inside = s > 0
            if r == 3:
                inside = s < NZ * NX - 1
            if c == 0:
                inside = (y > 0) if inside is None else inside & (y > 0)
            if c == 5:
                inside = (y < NY - 1) if inside is None else inside & (y < NY - 1)
            if inside is not None:
                v = v * inside.astype(F32)
            v = v.astype(BF16)
            act_ref[2, r, c] = v
            e = bdot(earlier, v).astype(BF16)
            act_ref[0, r, c] = e[:T]
            act_ref[1, r, c] = e[T:]


def convolve(own_columns, at_ref, act_ref, *refs):
    weights, out_ref = refs[:-1], refs[-1]
    core = at_ref[1]
    column = 2 * core if own_columns else 2 - 2 * core
    total = None
    for tap in range(27):
        j, a, b = tap // 9, tap // 3 % 3, tap % 3
        lhs = act_ref[j, a : a + 2, pl.ds(column + b, 2)].reshape(4 * T, HALF)
        rows = jnp.concatenate([v[i, tap] for v in weights for i in range(2)], axis=0)
        term = bdot(lhs, rows)
        total = term if total is None else total + term
    out_ref[...] = total.reshape(2, 2, T, CO)


def finish(order_ref, scale_ref, bias_ref, a_ref, b_ref, out_ref):
    picked = (iota((T, T), 0) == order_ref[...]).astype(F32).astype(BF16)
    for r in range(2):
        for c in range(2):
            v = ((a_ref[r, c] + b_ref[r, c]) * scale_ref[...] + bias_ref[...]).astype(BF16)
            v = lax.dot_general(picked, v, (((0,), (0,)), ((), ())), preferred_element_type=F32)
            at = (2 * r + c) * CO
            out_ref[:, at : at + CO] = v.astype(BF16)


def shift(value, step):
    pairs = []
    for i in range(NY * NC * NZ * NX):
        y, core, z, x = i // 64, i // 32 % 2, i // 4 % 8, i % 4
        to = step(y, core, z, x)
        if to is not None:
            ty, tc, tz, tx = to
            pairs.append((i, ((ty * NC + tc) * NZ + tz % NZ) * NX + tx))
    return lax.ppermute(value, AXES, pairs)


def by_space(y, core, s):
    return (y, core, s // NX, s % NX) if 0 <= s < NZ * NX else None


def struct(shape, dtype):
    return jax.ShapeDtypeStruct(shape, dtype)


def params(mib=48):
    return pltpu.CompilerParams(vmem_limit_bytes=mib * 2**20)


def cost(flops, size):
    return pl.CostEstimate(flops=flops, bytes_accessed=size, transcendentals=0)


def call_prepare(latent, weights):
    beside = struct((SHARD + 2 * EDGE, CO), BF16)
    return pl.pallas_call(
        prepare, out_shape=(struct((NZ * NX, 8, 128), F32), beside, beside), in_specs=[ANY, VMEM],
        out_specs=(VMEM, VMEM, VMEM),
        scratch_shapes=[pltpu.VMEM((FR, 2, W, C), BF16), pltpu.SemaphoreType.DMA((FR,))],
        compiler_params=params(60), cost_estimate=cost(2**16, 2**16),
    )(latent, weights)


def call_pack(*args):
    return pl.pallas_call(
        pack, out_shape=struct((SLABS, 112, HALF), BF16), in_specs=[SMEM] + [VMEM] * 5, out_specs=VMEM,
        compiler_params=params(), cost_estimate=cost(2**16, 2**16),
    )(*args)


def call_activate(*args):
    return pl.pallas_call(
        activate, out_shape=struct((3, 4, 6, T, HALF), BF16), in_specs=[SMEM, SMEM] + [VMEM] * 4, out_specs=VMEM,
        compiler_params=params(), cost_estimate=cost(2**16, 2**16),
    )(*args)


def call_finish(*args):
    return pl.pallas_call(
        finish, out_shape=struct((T, 4 * CO), BF16), in_specs=[VMEM] * 5, out_specs=VMEM, compiler_params=params(),
        cost_estimate=cost(2**22, 2**20),
    )(*args)


def local(latent, gamma, beta, smooth, weights, w_scale, bias, lengths, order):
    y, core, z, x = (lax.axis_index(a) for a in AXES)
    at = jnp.stack([y, core, z * NX + x]).astype(jnp.int32)
    latent = latent[0]
    weights = weights.reshape(27, GW, CO)

    spread, to_next, to_prev = call_prepare(latent, weights)

    def ring(v):
        return shift(v, lambda y, core, z, x: (y, core, z + 1 - 2 * core, x))

    def along(v, *d):
        return shift(v, lambda y, core, z, x: by_space(y, core, (z * NX + x - d[core]) % (NZ * NX)))

    def shard(v):
        return v[:SHARD].reshape(27, GW, CO)

    n1, n2, n3 = along(to_prev, 1, 2), along(to_next, -1, -1), along(to_prev, 2, 1)
    gathered = lax.all_to_all(spread, ("z", "x"), 0, 0, tiled=True)
    a0 = jnp.where(core == 0, jnp.stack([weights, shard(n1)]), jnp.stack([shard(n1), shard(n2)]))
    b0 = jnp.where(core == 0, jnp.stack([shard(n2), shard(n3)]), jnp.stack([weights, shard(n3)]))
    a1, b1 = ring(a0), ring(b0)
    windows = call_pack(at, latent, n2, n1, n3, gathered)
    columns = lax.all_to_all(windows, ("y", "core"), 0, 0, tiled=True)
    a2, b2 = ring(lax.optimization_barrier((a1, b1))[0]), ring(b1)
    a3, b3 = ring(a2), ring(b2)
    act = call_activate(at, lengths, gamma[None], beta[None], smooth[None], columns)
    a4 = ring(a3)


    def part(own_columns):
        return pl.pallas_call(
            functools.partial(convolve, own_columns), out_shape=struct((2, 2, T, CO), F32),
            in_specs=[SMEM] + [VMEM] * 9, out_specs=VMEM, compiler_params=params(32), cost_estimate=cost(2**30, 2**16),
        )(at, act, a0, a1, b1, a2, b2, a3, b3, a4)

    other = shift(part(False), lambda y, core, z, x: (y, 1 - core, z, x))
    keep = part(True)
    out = call_finish(order[None], w_scale[None], bias[None], keep, other)
    return out.reshape(SLABS, FR, 2, 2, CO)


def solution(mesh):
    inner = Mesh(mesh.devices.reshape(NY, NC, NZ, NX), AXES)
    slab, space = ("y", "core"), ("z", "x")
    in_specs = (
        P(slab, None, space, None, None), P(), P(), P(), P(None, None, None, space, None), P(), P(), P(), P(),
    )
    out_specs = P(None, None, space, slab, None)
    return jax.shard_map(local, mesh=inner, in_specs=in_specs, out_specs=out_specs, check_vma=False)
```

```python
import functools
import jax
import jax.numpy as jnp
from jax import lax
from jax.experimental import pallas as pl
from jax.experimental.pallas import tpu as pltpu
from jax.sharding import Mesh, PartitionSpec as P

C = 512
CO = 256
GROUPS = 32
GW = C // GROUPS
FR = 4
W = 32
SLABS = 16
T = FR * SLABS
HALF = C // 2
SHARD = 27 * GW
EDGE = FR * W
NY, NC, NZ, NX = 8, 2, 8, 4
AXES = ("y", "core", "z", "x")
HIGH = lax.Precision.HIGHEST
F32 = jnp.float32
BF16 = jnp.bfloat16
CELLS = 64 * GW
FRAME_CELLS = CELLS * NZ * NX
VMEM = pl.BlockSpec(memory_space=pltpu.VMEM)
SMEM = pl.BlockSpec(memory_space=pltpu.SMEM)
ANY = pl.BlockSpec(memory_space=pl.ANY)


def iota(shape, dim):
    return lax.broadcasted_iota(jnp.int32, shape, dim)


def group_of(shape, channel_dim, group_dim):
    return flag((iota(shape, channel_dim) >> 4) == iota(shape, group_dim))


def flag(condition):
    return condition.astype(F32).astype(BF16)


def bdot(a, b):
    return jnp.dot(a, b, preferred_element_type=F32)


def in_three(v):
    high = v.astype(BF16)
    rest = v - high.astype(F32)
    middle = rest.astype(BF16)
    return high, middle, (rest - middle.astype(F32)).astype(BF16)


def take(v, picks):
    n = v.shape[0]
    pad = -n % 8
    parts = [jnp.concatenate([p.astype(F32), jnp.zeros((pad, v.shape[1]), F32)], axis=0) for p in in_three(v)]
    out = bdot(jnp.concatenate(parts, axis=0).astype(BF16), picks)
    return out[:n] + out[n + pad : 2 * n + pad] + out[2 * (n + pad) : 3 * n + 2 * pad]


def prepare(x_hbm, w_ref, sums_ref, beside_ref, edge_ref, x_ref, sem):
    loads = [pltpu.make_async_copy(x_hbm.at[f], x_ref.at[f], sem.at[f]) for f in range(FR)]
    for copy in loads:
        copy.start()
    beside_ref[:SHARD] = w_ref[...].reshape(SHARD, CO)
    to_groups, to_channels = group_of((C, 128), 0, 1), group_of((128, C), 1, 0)
    rows = []
    for f in range(FR):
        loads[f].wait()
        rows.append(x_ref[f].reshape(2 * W, C).astype(F32))
    totals = jnp.concatenate([jnp.sum(v, axis=0, keepdims=True) for v in rows], axis=0)
    mean = take(totals, to_groups) * (1.0 / CELLS)
    spread = take(mean, to_channels)
    squares = []
    for f in range(FR):
        d = rows[f] - spread[f : f + 1]
        squares.append(jnp.sum(d * d, axis=0, keepdims=True))
    squares = take(jnp.concatenate(squares, axis=0), to_groups)
    core = lax.axis_index("core")
    edge = x_ref[:, core].reshape(EDGE, C)
    beside_ref[SHARD : SHARD + EDGE] = edge[:, :HALF]
    beside_ref[SHARD + EDGE :] = edge[:, HALF:]
    edge_ref[...] = x_ref[:, 1 - core].reshape(EDGE, C)
    sums_ref[...] = jnp.broadcast_to(jnp.concatenate([mean, squares], axis=0)[None], sums_ref.shape)


def join_space(v):
    n = NZ * NX
    mean = jnp.sum(v[:, :FR], axis=0) * (1.0 / n)
    d = v[:, :FR] - mean[None]
    squares = jnp.sum(v[:, FR:], axis=0) + CELLS * jnp.sum(d * d, axis=0)
    return jnp.concatenate([mean, squares], axis=0)


def channel_at(s, core, place):
    step = (place + 2 * GW) >> 6
    nth = jnp.where(step == 0, place >> 4, ((place >> 4) + 2) & 3)
    nth = (nth + 2 * core) & 3
    away = jnp.where(nth == 3, -1, nth)
    away = away + NX * jnp.where(core == 0, -step, step)
    return (((s + away) & (NZ * NX - 1)) << 4) + (place & 15)


def pack(own_ref, beside_ref, edge_ref, sums_ref, out_ref):
    core, s = lax.axis_index("core"), lax.axis_index("z") * NX + lax.axis_index("x")
    beside = jnp.concatenate([beside_ref[SHARD : SHARD + EDGE], beside_ref[SHARD + EDGE :]], axis=1)
    edge, first = edge_ref[...], core == 0
    up, down = jnp.where(first, edge, beside), jnp.where(first, beside, edge)
    source = jnp.concatenate([up, own_ref[...].reshape(2 * EDGE, C), down], axis=0)
    n = 4 * FR * W
    to = iota((n, 1), 0)
    col, row, frame = to >> 4, (to >> 2) & 3, to & 3
    want = jnp.where(
        row == 0,
        frame * W + col,
        jnp.where(row == 3, 3 * EDGE + frame * W + col, EDGE + (frame * 2 + row - 1) * W + col),
    )
    order = flag(want == iota((n, n), 1))
    place = iota((1, C), 1)
    roll = flag(iota((C, C), 0) == channel_at(s, place >> 8, place & (HALF - 1)))
    sorted_rows = bdot(order, source).astype(BF16)
    rolled = bdot(sorted_rows, roll).astype(BF16)
    sums = jnp.concatenate([join_space(sums_ref[...]), jnp.zeros((8, 128), F32)], axis=0)
    thirds = [p[:, :GROUPS] for p in in_three(sums)]
    thirds = jnp.concatenate(thirds + [jnp.zeros((16, HALF - 3 * GROUPS), BF16)], axis=1)
    for y in range(NY):
        for core in range(NC):
            lanes = slice(HALF * core, HALF * (core + 1))
            lo, hi = max(4 * y - 1, 0), min(4 * y + 5, W)
            first = lo - (4 * y - 1)
            out_ref[2 * y + core, 16 * first : 16 * (first + hi - lo), :] = rolled[16 * lo : 16 * hi, lanes]
            out_ref[2 * y + core, 96:112, :] = thirds
            if y == 0:
                out_ref[2 * y + core, 0:16, :] = jnp.zeros((16, HALF), BF16)
            if y == NY - 1:
                out_ref[2 * y + core, 80:96, :] = jnp.zeros((16, HALF), BF16)


def starts(lengths_ref, frame):
    end = lengths_ref[0]
    start = jnp.zeros_like(frame)
    for k in range(1, lengths_ref.shape[0]):
        start = jnp.where(frame >= end, end, start)
        end = end + lengths_ref[k]
    return start


def activate(lengths_ref, gamma_ref, beta_ref, smooth_ref, x_ref, act_ref):
    y, core, s = lax.axis_index("y"), lax.axis_index("core"), lax.axis_index("z") * NX + lax.axis_index("x")
    n = 2 * T
    thirds = x_ref[:, 96:112, :].astype(F32)[:, :8, :128].reshape(n, 128)
    rows, columns = iota((n, 1), 0), iota((1, n), 1)
    frame_a, frame_b = (rows >> 3) * FR + (rows & 3), (columns >> 3) * FR + (columns & 3)
    same = starts(lengths_ref, frame_a) == starts(lengths_ref, frame_b)
    means_b = (columns & 4) == 0
    on_means, on_squares = same & means_b, flag(same & jnp.logical_not(means_b))
    count = jnp.sum(on_means.astype(F32), axis=1, keepdims=True)
    on_means = flag(on_means)

    def whole(v):
        return v[:, :GROUPS] + v[:, GROUPS : 2 * GROUPS] + v[:, 2 * GROUPS : 3 * GROUPS]

    def parts(v):
        return jnp.concatenate(list(in_three(v)) + [jnp.zeros((n, 128 - 3 * GROUPS), BF16)], axis=1)

    mean = whole(bdot(on_means, thirds.astype(BF16))) / count
    off = whole(thirds) - mean
    squares = whole(bdot(on_squares, thirds.astype(BF16))) + FRAME_CELLS * whole(bdot(on_means, parts(off * off)))
    inverse = lax.rsqrt(squares / (count * FRAME_CELLS) + 1e-6)
    pick = flag((frame_b == iota((T, 1), 0)) & means_b)
    channels = channel_at(s, core, iota((1, HALF), 1))
    mine = flag(iota((C, HALF), 0) == channels)
    third = iota((128, 1), 0)
    to_group = flag(((third & (GROUPS - 1)) == (channels >> 4)) & (third < 3 * GROUPS))
    affine = take(jnp.concatenate([gamma_ref[...], beta_ref[...], smooth_ref[...]], axis=0), mine)
    gamma, beta, unsmooth = affine[0:1], affine[1:2], 1.0 / affine[2:3]
    mean = bdot(bdot(pick, parts(mean)).astype(BF16), to_group)
    scale = bdot(bdot(pick, parts(inverse)).astype(BF16), to_group) * gamma

    m = 16 * 16
    to = iota((m, 1), 0)
    row, t = to >> 6, to & (T - 1)
    by_row = flag(iota((m, m), 1) == (t >> 2) * 16 + row * FR + (t & 3))
    frame, other = iota((T, 1), 0), iota((T, T), 1)
    start = starts(lengths_ref, frame)
    earlier = [flag(other == jnp.maximum(frame - back, start)) for back in (2, 1)]
    earlier = jnp.concatenate(earlier, axis=0)
    for c in range(6):
        rows = x_ref[:, 16 * c : 16 * (c + 1), :].reshape(m, HALF)
        values = bdot(by_row, rows)
        for r in range(4):
            v = (values[T * r : T * (r + 1)] - mean) * scale + beta
            v = v / (1.0 + jnp.exp(-v)) * unsmooth
            inside = None
            if r == 0:
                inside = s > 0
            if r == 3:
                inside = s < NZ * NX - 1
            if c == 0:
                inside = (y > 0) if inside is None else inside & (y > 0)
            if c == 5:
                inside = (y < NY - 1) if inside is None else inside & (y < NY - 1)
            if inside is not None:
                v = v * inside.astype(F32)
            v = v.astype(BF16)
            act_ref[2, r, c] = v
            e = bdot(earlier, v).astype(BF16)
            act_ref[0, r, c] = e[:T]
            act_ref[1, r, c] = e[T:]


def convolve(own_columns, act_ref, *refs):
    weights, out_ref = refs[:-1], refs[-1]
    core = lax.axis_index("core")
    column = 2 * core if own_columns else 2 - 2 * core
    total = None
    for tap in range(27):
        j, a, b = tap // 9, tap // 3 % 3, tap % 3
        lhs = act_ref[j, a : a + 2, pl.ds(column + b, 2)].reshape(4 * T, HALF)
        rows = jnp.concatenate([v[i, tap] for v in weights for i in range(2)], axis=0)
        term = bdot(lhs, rows)
        total = term if total is None else total + term
    out_ref[...] = total.reshape(2, 2, T, CO)


def finish(order_ref, scale_ref, bias_ref, a_ref, b_ref, out_ref):
    picked = (iota((T, T), 0) == order_ref[...]).astype(F32).astype(BF16)
    for r in range(2):
        for c in range(2):
            v = ((a_ref[r, c] + b_ref[r, c]) * scale_ref[...] + bias_ref[...]).astype(BF16)
            v = lax.dot_general(picked, v, (((0,), (0,)), ((), ())), preferred_element_type=F32)
            at = (2 * r + c) * CO
            out_ref[:, at : at + CO] = v.astype(BF16)


def shift(value, step):
    pairs = []
    for i in range(NY * NC * NZ * NX):
        y, core, z, x = i // 64, i // 32 % 2, i // 4 % 8, i % 4
        to = step(y, core, z, x)
        if to is not None:
            ty, tc, tz, tx = to
            pairs.append((i, ((ty * NC + tc) * NZ + tz % NZ) * NX + tx))
    return lax.ppermute(value, AXES, pairs)


def by_space(y, core, s):
    return (y, core, s // NX, s % NX) if 0 <= s < NZ * NX else None


def struct(shape, dtype):
    return jax.ShapeDtypeStruct(shape, dtype)


def params(mib=48):
    return pltpu.CompilerParams(vmem_limit_bytes=mib * 2**20)


def cost(flops, size):
    return pl.CostEstimate(flops=flops, bytes_accessed=size, transcendentals=0)


def call_prepare(*args):
    return pl.pallas_call(
        prepare,
        out_shape=(
            struct((NZ * NX, 8, 128), F32), struct((SHARD + 2 * EDGE, CO), BF16), struct((EDGE, C), BF16)
        ),
        in_specs=[ANY, VMEM], out_specs=(VMEM, VMEM, VMEM),
        scratch_shapes=[pltpu.VMEM((FR, 2, W, C), BF16), pltpu.SemaphoreType.DMA((FR,))],
        compiler_params=params(60), cost_estimate=cost(2**16, 2**16),
    )(*args)


def call_pack(*args):
    return pl.pallas_call(
        pack, out_shape=struct((SLABS, 112, HALF), BF16), in_specs=[VMEM] * 4, out_specs=VMEM,
        compiler_params=params(), cost_estimate=cost(2**16, 2**16),
    )(*args)


def call_activate(*args):
    return pl.pallas_call(
        activate, out_shape=struct((3, 4, 6, T, HALF), BF16), in_specs=[SMEM] + [VMEM] * 4, out_specs=VMEM,
        compiler_params=params(), cost_estimate=cost(2**16, 2**16),
    )(*args)


def call_finish(*args):
    return pl.pallas_call(
        finish, out_shape=struct((T, 4 * CO), BF16), in_specs=[VMEM] * 5, out_specs=VMEM, compiler_params=params(),
        cost_estimate=cost(2**22, 2**20),
    )(*args)


def local(latent, gamma, beta, smooth, weights, w_scale, bias, lengths, order):
    core = lax.axis_index("core")
    latent = latent[0]
    weights = weights.reshape(27, GW, CO)

    spread, to_beside, edge = call_prepare(latent, weights)

    def ring(v):
        return shift(v, lambda y, core, z, x: (y, core, z + 1 - 2 * core, x))

    def along(v, *d):
        def step(y, core, z, x):
            return None if d[core] is None else by_space(y, core, (z * NX + x - d[core]) % (NZ * NX))

        return shift(v, step)

    def other_core(v):
        return shift(v, lambda y, core, z, x: (y, 1 - core, z, x))

    beside, second = along(to_beside, 1, -1), along(weights, None, 2)
    gathered = lax.all_to_all(spread, ("z", "x"), 0, 0, tiled=True)
    edge = along(edge, -1, 1)
    near = beside[:SHARD].reshape(27, GW, CO)
    a0 = jnp.where(core == 0, jnp.stack([weights, near]), jnp.stack([second, near]))
    b0 = other_core(a0)
    a1, b1 = ring(a0), ring(b0)
    windows = call_pack(latent, beside, edge, gathered)
    columns = lax.all_to_all(windows, ("y", "core"), 0, 0, tiled=True)
    a2, b2 = ring(a1), ring(b1)
    a3, b3 = ring(a2), ring(b2)
    act = call_activate(lengths, gamma[None], beta[None], smooth[None], columns)
    a4 = ring(a3)


    def part(own_columns):
        return pl.pallas_call(
            functools.partial(convolve, own_columns), out_shape=struct((2, 2, T, CO), F32),
            in_specs=[VMEM] * 9, out_specs=VMEM, compiler_params=params(32), cost_estimate=cost(2**30, 2**16),
        )(act, a0, a1, b1, a2, b2, a3, b3, a4)

    other = other_core(part(False))
    keep = part(True)
    out = call_finish(order[None], w_scale[None], bias[None], keep, other)
    return out.reshape(SLABS, FR, 2, 2, CO)


def solution(mesh):
    inner = Mesh(mesh.devices.reshape(NY, NC, NZ, NX), AXES)
    slab, space = ("y", "core"), ("z", "x")
    in_specs = (
        P(slab, None, space, None, None), P(), P(), P(), P(None, None, None, space, None), P(), P(), P(), P(),
    )
    out_specs = P(None, None, space, slab, None)
    return jax.shard_map(local, mesh=inner, in_specs=in_specs, out_specs=out_specs, check_vma=False)
```

```python
import functools
import jax
import jax.numpy as jnp
from jax import lax
from jax.experimental import pallas as pl
from jax.experimental.pallas import tpu as pltpu
from jax.sharding import Mesh, PartitionSpec as P

C = 512
CO = 256
GROUPS = 32
GW = C // GROUPS
FR = 4
W = 32
SLABS = 16
T = FR * SLABS
HALF = C // 2
SHARD = 27 * GW
EDGE = FR * W
NY, NC, NZ, NX = 8, 2, 8, 4
AXES = ("y", "core", "z", "x")
HIGH = lax.Precision.HIGHEST
F32 = jnp.float32
BF16 = jnp.bfloat16
CELLS = 64 * GW
FRAME_CELLS = CELLS * NZ * NX
VMEM = pl.BlockSpec(memory_space=pltpu.VMEM)
SMEM = pl.BlockSpec(memory_space=pltpu.SMEM)
ANY = pl.BlockSpec(memory_space=pl.ANY)


def iota(shape, dim):
    return lax.broadcasted_iota(jnp.int32, shape, dim)


def group_of(shape, channel_dim, group_dim):
    return flag((iota(shape, channel_dim) >> 4) == iota(shape, group_dim))


def flag(condition):
    return condition.astype(F32).astype(BF16)


def bdot(a, b):
    return jnp.dot(a, b, preferred_element_type=F32)


def in_three(v):
    high = v.astype(BF16)
    rest = v - high.astype(F32)
    middle = rest.astype(BF16)
    return high, middle, (rest - middle.astype(F32)).astype(BF16)


def take(v, picks):
    n = v.shape[0]
    pad = -n % 8
    parts = [jnp.concatenate([p.astype(F32), jnp.zeros((pad, v.shape[1]), F32)], axis=0) for p in in_three(v)]
    out = bdot(jnp.concatenate(parts, axis=0).astype(BF16), picks)
    return out[:n] + out[n + pad : 2 * n + pad] + out[2 * (n + pad) : 3 * n + 2 * pad]


def prepare(x_hbm, w_ref, sums_ref, beside_ref, edge_ref, x_ref, sem):
    loads = [pltpu.make_async_copy(x_hbm.at[f], x_ref.at[f], sem.at[f]) for f in range(FR)]
    for copy in loads:
        copy.start()
    beside_ref[:SHARD] = w_ref[...].reshape(SHARD, CO)
    to_groups, to_channels = group_of((C, 128), 0, 1), group_of((128, C), 1, 0)
    rows = []
    for f in range(FR):
        loads[f].wait()
        rows.append(x_ref[f].reshape(2 * W, C).astype(F32))
    totals = jnp.concatenate([jnp.sum(v, axis=0, keepdims=True) for v in rows], axis=0)
    mean = take(totals, to_groups) * (1.0 / CELLS)
    spread = take(mean, to_channels)
    squares = []
    for f in range(FR):
        d = rows[f] - spread[f : f + 1]
        squares.append(jnp.sum(d * d, axis=0, keepdims=True))
    squares = take(jnp.concatenate(squares, axis=0), to_groups)
    core = lax.axis_index("core")
    edge = x_ref[:, core].reshape(EDGE, C)
    beside_ref[SHARD : SHARD + EDGE] = edge[:, :HALF]
    beside_ref[SHARD + EDGE :] = edge[:, HALF:]
    edge_ref[...] = x_ref[:, 1 - core].reshape(EDGE, C)
    sums_ref[...] = jnp.broadcast_to(jnp.concatenate([mean, squares], axis=0)[None], sums_ref.shape)


def join_space(v):
    n = NZ * NX
    mean = jnp.sum(v[:, :FR], axis=0) * (1.0 / n)
    d = v[:, :FR] - mean[None]
    squares = jnp.sum(v[:, FR:], axis=0) + CELLS * jnp.sum(d * d, axis=0)
    return jnp.concatenate([mean, squares], axis=0)


def channel_at(s, core, place):
    step = (place + 2 * GW) >> 6
    nth = jnp.where(step == 0, place >> 4, ((place >> 4) + 2) & 3)
    nth = (nth + 2 * core) & 3
    away = jnp.where(nth == 3, -1, nth)
    away = away + NX * jnp.where(core == 0, -step, step)
    return (((s + away) & (NZ * NX - 1)) << 4) + (place & 15)


def pack(own_ref, beside_ref, edge_ref, sums_ref, out_ref):
    core, s = lax.axis_index("core"), lax.axis_index("z") * NX + lax.axis_index("x")
    beside = jnp.concatenate([beside_ref[SHARD : SHARD + EDGE], beside_ref[SHARD + EDGE :]], axis=1)
    edge, first = edge_ref[...], core == 0
    up, down = jnp.where(first, edge, beside), jnp.where(first, beside, edge)
    source = jnp.concatenate([up, own_ref[...].reshape(2 * EDGE, C), down], axis=0)
    n = 4 * FR * W
    to = iota((n, 1), 0)
    col, row, frame = to >> 4, (to >> 2) & 3, to & 3
    want = jnp.where(
        row == 0,
        frame * W + col,
        jnp.where(row == 3, 3 * EDGE + frame * W + col, EDGE + (frame * 2 + row - 1) * W + col),
    )
    order = flag(want == iota((n, n), 1))
    place = iota((1, C), 1)
    roll = flag(iota((C, C), 0) == channel_at(s, place >> 8, place & (HALF - 1)))
    sorted_rows = bdot(order, source).astype(BF16)
    rolled = bdot(sorted_rows, roll).astype(BF16)
    sums = jnp.concatenate([join_space(sums_ref[...]), jnp.zeros((8, 128), F32)], axis=0)
    thirds = [p[:, :GROUPS] for p in in_three(sums)]
    thirds = jnp.concatenate(thirds + [jnp.zeros((16, HALF - 3 * GROUPS), BF16)], axis=1)
    for y in range(NY):
        for core in range(NC):
            lanes = slice(HALF * core, HALF * (core + 1))
            lo, hi = max(4 * y - 1, 0), min(4 * y + 5, W)
            first = lo - (4 * y - 1)
            out_ref[2 * y + core, 16 * first : 16 * (first + hi - lo), :] = rolled[16 * lo : 16 * hi, lanes]
            out_ref[2 * y + core, 96:112, :] = thirds
            if y == 0:
                out_ref[2 * y + core, 0:16, :] = jnp.zeros((16, HALF), BF16)
            if y == NY - 1:
                out_ref[2 * y + core, 80:96, :] = jnp.zeros((16, HALF), BF16)


def starts(lengths_ref, frame):
    end = lengths_ref[0]
    start = jnp.zeros_like(frame)
    for k in range(1, lengths_ref.shape[0]):
        start = jnp.where(frame >= end, end, start)
        end = end + lengths_ref[k]
    return start


def activate(lengths_ref, gamma_ref, beta_ref, smooth_ref, x_ref, act_ref):
    y, core, s = lax.axis_index("y"), lax.axis_index("core"), lax.axis_index("z") * NX + lax.axis_index("x")
    n = 2 * T
    thirds = x_ref[:, 96:112, :].astype(F32)[:, :8, :128].reshape(n, 128)
    rows, columns = iota((n, 1), 0), iota((1, n), 1)
    frame_a, frame_b = (rows >> 3) * FR + (rows & 3), (columns >> 3) * FR + (columns & 3)
    same = starts(lengths_ref, frame_a) == starts(lengths_ref, frame_b)
    means_b = (columns & 4) == 0
    on_means, on_squares = same & means_b, flag(same & jnp.logical_not(means_b))
    count = jnp.sum(on_means.astype(F32), axis=1, keepdims=True)
    on_means = flag(on_means)

    def whole(v):
        return v[:, :GROUPS] + v[:, GROUPS : 2 * GROUPS] + v[:, 2 * GROUPS : 3 * GROUPS]

    def parts(v):
        return jnp.concatenate(list(in_three(v)) + [jnp.zeros((n, 128 - 3 * GROUPS), BF16)], axis=1)

    mean = whole(bdot(on_means, thirds.astype(BF16))) / count
    off = whole(thirds) - mean
    squares = whole(bdot(on_squares, thirds.astype(BF16))) + FRAME_CELLS * whole(bdot(on_means, parts(off * off)))
    inverse = lax.rsqrt(squares / (count * FRAME_CELLS) + 1e-6)
    pick = flag((frame_b == iota((T, 1), 0)) & means_b)
    channels = channel_at(s, core, iota((1, HALF), 1))
    mine = flag(iota((C, HALF), 0) == channels)
    third = iota((128, 1), 0)
    to_group = flag(((third & (GROUPS - 1)) == (channels >> 4)) & (third < 3 * GROUPS))
    affine = take(jnp.concatenate([gamma_ref[...], beta_ref[...], smooth_ref[...]], axis=0), mine)
    gamma, beta, unsmooth = affine[0:1], affine[1:2], 1.0 / affine[2:3]
    mean = bdot(bdot(pick, parts(mean)).astype(BF16), to_group)
    scale = bdot(bdot(pick, parts(inverse)).astype(BF16), to_group) * gamma

    m = 16 * 16
    to = iota((m, 1), 0)
    row, t = to >> 6, to & (T - 1)
    by_row = flag(iota((m, m), 1) == (t >> 2) * 16 + row * FR + (t & 3))
    frame, other = iota((T, 1), 0), iota((T, T), 1)
    start = starts(lengths_ref, frame)
    earlier = [flag(other == jnp.maximum(frame - back, start)) for back in (2, 1)]
    earlier = jnp.concatenate(earlier, axis=0)
    for c in range(6):
        rows = x_ref[:, 16 * c : 16 * (c + 1), :].reshape(m, HALF)
        values = bdot(by_row, rows)
        for r in range(4):
            v = (values[T * r : T * (r + 1)] - mean) * scale + beta
            v = v / (1.0 + jnp.exp(-v)) * unsmooth
            inside = None
            if r == 0:
                inside = s > 0
            if r == 3:
                inside = s < NZ * NX - 1
            if c == 0:
                inside = (y > 0) if inside is None else inside & (y > 0)
            if c == 5:
                inside = (y < NY - 1) if inside is None else inside & (y < NY - 1)
            if inside is not None:
                v = v * inside.astype(F32)
            v = v.astype(BF16)
            act_ref[2, r, c] = v
            e = bdot(earlier, v).astype(BF16)
            act_ref[0, r, c] = e[:T]
            act_ref[1, r, c] = e[T:]


def convolve(own_columns, act_ref, *refs):
    weights, out_ref = refs[:-1], refs[-1]
    core = lax.axis_index("core")
    column = 2 * core if own_columns else 2 - 2 * core
    total = None
    for tap in range(27):
        j, a, b = tap // 9, tap // 3 % 3, tap % 3
        lhs = act_ref[j, a : a + 2, pl.ds(column + b, 2)].reshape(4 * T, HALF)
        rows = jnp.concatenate([v[i, tap] for v in weights for i in range(2)], axis=0)
        term = bdot(lhs, rows)
        total = term if total is None else total + term
    out_ref[...] = total.reshape(2, 2, T, CO)


def finish(order_ref, scale_ref, bias_ref, a_ref, b_ref, out_ref):
    picked = (iota((T, T), 0) == order_ref[...]).astype(F32).astype(BF16)
    for r in range(2):
        for c in range(2):
            v = ((a_ref[r, c] + b_ref[r, c]) * scale_ref[...] + bias_ref[...]).astype(BF16)
            v = lax.dot_general(picked, v, (((0,), (0,)), ((), ())), preferred_element_type=F32)
            at = (2 * r + c) * CO
            out_ref[:, at : at + CO] = v.astype(BF16)


def shift(value, step):
    pairs = []
    for i in range(NY * NC * NZ * NX):
        y, core, z, x = i // 64, i // 32 % 2, i // 4 % 8, i % 4
        to = step(y, core, z, x)
        if to is not None:
            ty, tc, tz, tx = to
            pairs.append((i, ((ty * NC + tc) * NZ + tz % NZ) * NX + tx))
    return lax.ppermute(value, AXES, pairs)


def by_space(y, core, s):
    return (y, core, s // NX, s % NX) if 0 <= s < NZ * NX else None


def struct(shape, dtype):
    return jax.ShapeDtypeStruct(shape, dtype)


def params(mib=48):
    return pltpu.CompilerParams(vmem_limit_bytes=mib * 2**20)


def cost(flops, size):
    return pl.CostEstimate(flops=flops, bytes_accessed=size, transcendentals=0)


def call_prepare(*args):
    return pl.pallas_call(
        prepare,
        out_shape=(
            struct((NZ * NX, 8, 128), F32), struct((SHARD + 2 * EDGE, CO), BF16), struct((EDGE, C), BF16)
        ),
        in_specs=[ANY, VMEM], out_specs=(VMEM, VMEM, VMEM),
        scratch_shapes=[pltpu.VMEM((FR, 2, W, C), BF16), pltpu.SemaphoreType.DMA((FR,))],
        compiler_params=params(60), cost_estimate=cost(2**16, 2**16),
    )(*args)


def call_pack(*args):
    return pl.pallas_call(
        pack, out_shape=struct((SLABS, 112, HALF), BF16), in_specs=[VMEM] * 4, out_specs=VMEM,
        compiler_params=params(), cost_estimate=cost(2**16, 2**16),
    )(*args)


def call_activate(*args):
    return pl.pallas_call(
        activate, out_shape=struct((3, 4, 6, T, HALF), BF16), in_specs=[SMEM] + [VMEM] * 4, out_specs=VMEM,
        compiler_params=params(), cost_estimate=cost(2**16, 2**16),
    )(*args)


def call_finish(*args):
    return pl.pallas_call(
        finish, out_shape=struct((T, 4 * CO), BF16), in_specs=[VMEM] * 5, out_specs=VMEM, compiler_params=params(),
        cost_estimate=cost(2**22, 2**20),
    )(*args)


def local(latent, gamma, beta, smooth, weights, w_scale, bias, lengths, order):
    core = lax.axis_index("core")
    latent = latent[0]
    weights = weights.reshape(27, GW, CO)

    spread, to_beside, edge = call_prepare(latent, weights)

    def ring(v):
        return shift(v, lambda y, core, z, x: (y, core, z + 1 - 2 * core, x))

    def along(v, *d):
        def step(y, core, z, x):
            return None if d[core] is None else by_space(y, core, (z * NX + x - d[core]) % (NZ * NX))

        return shift(v, step)

    def other_core(v):
        return shift(v, lambda y, core, z, x: (y, 1 - core, z, x))

    beside, second = along(to_beside, 1, -1), along(weights, None, 2)
    gathered = lax.all_to_all(spread, ("z", "x"), 0, 0, tiled=True)
    edge = along(edge, -1, 1)
    near = beside[:SHARD].reshape(27, GW, CO)
    a0 = jnp.where(core == 0, jnp.stack([weights, near]), jnp.stack([second, near]))
    a1 = ring(a0)
    b1 = shift(a0, lambda y, core, z, x: (y, 1 - core, z - 1 + 2 * core, x))
    windows = call_pack(latent, beside, edge, gathered)
    columns = lax.all_to_all(windows, ("y", "core"), 0, 0, tiled=True)
    a2, b2 = ring(lax.optimization_barrier((a1, b1))[0]), ring(b1)
    a3, b3 = ring(a2), ring(b2)
    act = call_activate(lengths, gamma[None], beta[None], smooth[None], columns)
    a4 = ring(a3)


    def part(own_columns):
        return pl.pallas_call(
            functools.partial(convolve, own_columns), out_shape=struct((2, 2, T, CO), F32),
            in_specs=[VMEM] * 9, out_specs=VMEM, compiler_params=params(32), cost_estimate=cost(2**30, 2**16),
        )(act, a0, a1, b1, a2, b2, a3, b3, a4)

    other = other_core(part(False))
    keep = part(True)
    out = call_finish(order[None], w_scale[None], bias[None], keep, other)
    return out.reshape(SLABS, FR, 2, 2, CO)


def solution(mesh):
    inner = Mesh(mesh.devices.reshape(NY, NC, NZ, NX), AXES)
    slab, space = ("y", "core"), ("z", "x")
    in_specs = (
        P(slab, None, space, None, None), P(), P(), P(), P(None, None, None, space, None), P(), P(), P(), P(),
    )
    out_specs = P(None, None, space, slab, None)
    return jax.shard_map(local, mesh=inner, in_specs=in_specs, out_specs=out_specs, check_vma=False)
```

```python
import functools
import jax
import jax.numpy as jnp
from jax import lax
from jax.experimental import pallas as pl
from jax.experimental.pallas import tpu as pltpu
from jax.sharding import Mesh, PartitionSpec as P

C = 512
CO = 256
GROUPS = 32
GW = C // GROUPS
FR = 4
W = 32
SLABS = 16
T = FR * SLABS
HALF = C // 2
LAST = 384
SHARD = 27 * GW
EDGE = FR * W
NY, NC, NZ, NX = 8, 2, 8, 4
AXES = ("y", "core", "z", "x")
HIGH = lax.Precision.HIGHEST
F32 = jnp.float32
BF16 = jnp.bfloat16
CELLS = 64 * GW
FRAME_CELLS = CELLS * NZ * NX
VMEM = pl.BlockSpec(memory_space=pltpu.VMEM)
SMEM = pl.BlockSpec(memory_space=pltpu.SMEM)
ANY = pl.BlockSpec(memory_space=pl.ANY)


def iota(shape, dim):
    return lax.broadcasted_iota(jnp.int32, shape, dim)


def group_of(shape, channel_dim, group_dim):
    return flag((iota(shape, channel_dim) >> 4) == iota(shape, group_dim))


def flag(condition):
    return condition.astype(F32).astype(BF16)


def bdot(a, b):
    return jnp.dot(a, b, preferred_element_type=F32)


def in_three(v):
    high = v.astype(BF16)
    rest = v - high.astype(F32)
    middle = rest.astype(BF16)
    return high, middle, (rest - middle.astype(F32)).astype(BF16)


def take(v, picks):
    n = v.shape[0]
    pad = -n % 8
    parts = [jnp.concatenate([p.astype(F32), jnp.zeros((pad, v.shape[1]), F32)], axis=0) for p in in_three(v)]
    out = bdot(jnp.concatenate(parts, axis=0).astype(BF16), picks)
    return out[:n] + out[n + pad : 2 * n + pad] + out[2 * (n + pad) : 3 * n + 2 * pad]


def prepare(x_hbm, w_ref, sums_ref, beside_ref, edge_ref, x_ref, sem):
    loads = [pltpu.make_async_copy(x_hbm.at[f], x_ref.at[f], sem.at[f]) for f in range(FR)]
    for copy in loads:
        copy.start()
    beside_ref[:SHARD] = w_ref[...].reshape(SHARD, CO)
    to_groups, to_channels = group_of((C, 128), 0, 1), group_of((128, C), 1, 0)
    rows = []
    for f in range(FR):
        loads[f].wait()
        rows.append(x_ref[f].reshape(2 * W, C).astype(F32))
    totals = jnp.concatenate([jnp.sum(v, axis=0, keepdims=True) for v in rows], axis=0)
    mean = take(totals, to_groups) * (1.0 / CELLS)
    spread = take(mean, to_channels)
    squares = []
    for f in range(FR):
        d = rows[f] - spread[f : f + 1]
        squares.append(jnp.sum(d * d, axis=0, keepdims=True))
    squares = take(jnp.concatenate(squares, axis=0), to_groups)
    core = lax.axis_index("core")
    edge = x_ref[:, core].reshape(EDGE, C)
    beside_ref[SHARD : SHARD + EDGE] = edge[:, :HALF]
    beside_ref[SHARD + EDGE :] = edge[:, HALF:]
    edge_ref[...] = x_ref[:, 1 - core].reshape(EDGE, C)
    sums_ref[...] = jnp.broadcast_to(jnp.concatenate([mean, squares], axis=0)[None], sums_ref.shape)


def join_space(v):
    n = NZ * NX
    mean = jnp.sum(v[:, :FR], axis=0) * (1.0 / n)
    d = v[:, :FR] - mean[None]
    squares = jnp.sum(v[:, FR:], axis=0) + CELLS * jnp.sum(d * d, axis=0)
    return jnp.concatenate([mean, squares], axis=0)


def channel_at(s, core, place):
    step = (place + 2 * GW) >> 6
    nth = jnp.where(step == 0, place >> 4, ((place >> 4) + 2) & 3)
    nth = (nth + 2 * core) & 3
    away = jnp.where(nth == 3, -1, nth)
    away = away + NX * jnp.where(core == 0, -step, step)
    return (((s + away) & (NZ * NX - 1)) << 4) + (place & 15)


def pack(own_ref, beside_ref, edge_ref, sums_ref, out_ref):
    core, s = lax.axis_index("core"), lax.axis_index("z") * NX + lax.axis_index("x")
    beside = jnp.concatenate([beside_ref[SHARD : SHARD + EDGE], beside_ref[SHARD + EDGE :]], axis=1)
    edge, first = edge_ref[...], core == 0
    up, down = jnp.where(first, edge, beside), jnp.where(first, beside, edge)
    source = jnp.concatenate([up, own_ref[...].reshape(2 * EDGE, C), down], axis=0)
    n = 4 * FR * W
    to = iota((n, 1), 0)
    col, row, frame = to >> 4, (to >> 2) & 3, to & 3
    want = jnp.where(
        row == 0,
        frame * W + col,
        jnp.where(row == 3, 3 * EDGE + frame * W + col, EDGE + (frame * 2 + row - 1) * W + col),
    )
    order = flag(want == iota((n, n), 1))
    place = iota((1, C), 1)
    roll = flag(iota((C, C), 0) == channel_at(s, place >> 8, place & (HALF - 1)))
    sorted_rows = bdot(order, source).astype(BF16)
    rolled = bdot(sorted_rows, roll).astype(BF16)
    sums = jnp.concatenate([join_space(sums_ref[...]), jnp.zeros((8, 128), F32)], axis=0)
    thirds = [p[:, :GROUPS] for p in in_three(sums)]
    thirds = jnp.concatenate(thirds + [jnp.zeros((16, HALF - 3 * GROUPS), BF16)], axis=1)
    for y in range(NY):
        for core in range(NC):
            lanes = slice(HALF * core, HALF * (core + 1))
            lo, hi = max(4 * y - 1, 0), min(4 * y + 5, W)
            first = lo - (4 * y - 1)
            out_ref[2 * y + core, 16 * first : 16 * (first + hi - lo), :] = rolled[16 * lo : 16 * hi, lanes]
            out_ref[2 * y + core, 96:112, :] = thirds
            if y == 0:
                out_ref[2 * y + core, 0:16, :] = jnp.zeros((16, HALF), BF16)
            if y == NY - 1:
                out_ref[2 * y + core, 80:96, :] = jnp.zeros((16, HALF), BF16)


def starts(lengths_ref, frame):
    end = lengths_ref[0]
    start = jnp.zeros_like(frame)
    for k in range(1, lengths_ref.shape[0]):
        start = jnp.where(frame >= end, end, start)
        end = end + lengths_ref[k]
    return start


def activate(lengths_ref, gamma_ref, beta_ref, smooth_ref, x_ref, act_ref, last_ref):
    y, core, s = lax.axis_index("y"), lax.axis_index("core"), lax.axis_index("z") * NX + lax.axis_index("x")
    n = 2 * T
    thirds = x_ref[:, 96:112, :].astype(F32)[:, :8, :128].reshape(n, 128)
    rows, columns = iota((n, 1), 0), iota((1, n), 1)
    frame_a, frame_b = (rows >> 3) * FR + (rows & 3), (columns >> 3) * FR + (columns & 3)
    same = starts(lengths_ref, frame_a) == starts(lengths_ref, frame_b)
    means_b = (columns & 4) == 0
    on_means, on_squares = same & means_b, flag(same & jnp.logical_not(means_b))
    count = jnp.sum(on_means.astype(F32), axis=1, keepdims=True)
    on_means = flag(on_means)

    def whole(v):
        return v[:, :GROUPS] + v[:, GROUPS : 2 * GROUPS] + v[:, 2 * GROUPS : 3 * GROUPS]

    def parts(v):
        return jnp.concatenate(list(in_three(v)) + [jnp.zeros((n, 128 - 3 * GROUPS), BF16)], axis=1)

    mean = whole(bdot(on_means, thirds.astype(BF16))) / count
    off = whole(thirds) - mean
    squares = whole(bdot(on_squares, thirds.astype(BF16))) + FRAME_CELLS * whole(bdot(on_means, parts(off * off)))
    inverse = lax.rsqrt(squares / (count * FRAME_CELLS) + 1e-6)
    pick = flag((frame_b == iota((T, 1), 0)) & means_b)
    channels = channel_at(s, core, iota((1, HALF), 1))
    mine = flag(iota((C, HALF), 0) == channels)
    third = iota((128, 1), 0)
    to_group = flag(((third & (GROUPS - 1)) == (channels >> 4)) & (third < 3 * GROUPS))
    affine = take(jnp.concatenate([gamma_ref[...], beta_ref[...], smooth_ref[...]], axis=0), mine)
    gamma, beta, unsmooth = affine[0:1], affine[1:2], 1.0 / affine[2:3]
    mean = bdot(bdot(pick, parts(mean)).astype(BF16), to_group)
    scale = bdot(bdot(pick, parts(inverse)).astype(BF16), to_group) * gamma

    m = 16 * 16
    to = iota((m, 1), 0)
    row, t = to >> 6, to & (T - 1)
    by_row = flag(iota((m, m), 1) == (t >> 2) * 16 + row * FR + (t & 3))
    frame, other = iota((T, 1), 0), iota((T, T), 1)
    start = starts(lengths_ref, frame)
    earlier = [flag(other == jnp.maximum(frame - back, start)) for back in (2, 1)]
    earlier = jnp.concatenate(earlier, axis=0)
    for c in range(6):
        rows = x_ref[:, 16 * c : 16 * (c + 1), :].reshape(m, HALF)
        values = bdot(by_row, rows)
        for r in range(4):
            v = (values[T * r : T * (r + 1)] - mean) * scale + beta
            v = v / (1.0 + jnp.exp(-v)) * unsmooth
            inside = None
            if r == 0:
                inside = s > 0
            if r == 3:
                inside = s < NZ * NX - 1
            if c == 0:
                inside = (y > 0) if inside is None else inside & (y > 0)
            if c == 5:
                inside = (y < NY - 1) if inside is None else inside & (y < NY - 1)
            if inside is not None:
                v = v * inside.astype(F32)
            v = v.astype(BF16)
            act_ref[2, r, c] = v
            e = bdot(earlier, v).astype(BF16)
            act_ref[0, r, c] = e[:T]
            act_ref[1, r, c] = e[T:]
    for r in range(4):
        for c in range(4):
            taps = [act_ref[j, r, c + b, :, HALF - 2 * GW :] for j in range(3) for b in range(3)]
            last_ref[r, c] = jnp.concatenate(taps + [jnp.zeros((T, LAST - 18 * GW), BF16)], axis=1)


def convolve(own_columns, act_ref, *refs):
    weights, out_ref = refs[:-1], refs[-1]
    core = lax.axis_index("core")
    column = 2 * core if own_columns else 2 - 2 * core
    total = None
    for tap in range(27):
        j, a, b = tap // 9, tap // 3 % 3, tap % 3
        lhs = act_ref[j, a : a + 2, pl.ds(column + b, 2)].reshape(4 * T, HALF)
        rows = jnp.concatenate([v[i, tap] for v in weights for i in range(2)], axis=0)
        term = bdot(lhs[:, : rows.shape[0]], rows)
        total = term if total is None else total + term
    out_ref[...] = total.reshape(2, 2, T, CO)


def complete(last_ref, w_ref, part_ref, out_ref):
    column = 2 - 2 * lax.axis_index("core")
    total = part_ref[...].reshape(4 * T, CO)
    for a in range(3):
        lhs = last_ref[a : a + 2, pl.ds(column, 2)].reshape(4 * T, LAST)
        rows = [w_ref[i, 9 * j + 3 * a + b] for j in range(3) for b in range(3) for i in range(2)]
        total = total + bdot(lhs, jnp.concatenate(rows + [jnp.zeros((LAST - 18 * GW, CO), BF16)], axis=0))
    out_ref[...] = total.reshape(2, 2, T, CO)


def finish(order_ref, scale_ref, bias_ref, a_ref, b_ref, out_ref):
    picked = (iota((T, T), 0) == order_ref[...]).astype(F32).astype(BF16)
    for r in range(2):
        for c in range(2):
            v = ((a_ref[r, c] + b_ref[r, c]) * scale_ref[...] + bias_ref[...]).astype(BF16)
            v = lax.dot_general(picked, v, (((0,), (0,)), ((), ())), preferred_element_type=F32)
            at = (2 * r + c) * CO
            out_ref[:, at : at + CO] = v.astype(BF16)


def shift(value, step):
    pairs = []
    for i in range(NY * NC * NZ * NX):
        y, core, z, x = i // 64, i // 32 % 2, i // 4 % 8, i % 4
        to = step(y, core, z, x)
        if to is not None:
            ty, tc, tz, tx = to
            pairs.append((i, ((ty * NC + tc) * NZ + tz % NZ) * NX + tx))
    return lax.ppermute(value, AXES, pairs)


def by_space(y, core, s):
    return (y, core, s // NX, s % NX) if 0 <= s < NZ * NX else None


def struct(shape, dtype):
    return jax.ShapeDtypeStruct(shape, dtype)


def params(mib=48):
    return pltpu.CompilerParams(vmem_limit_bytes=mib * 2**20)


def cost(flops, size):
    return pl.CostEstimate(flops=flops, bytes_accessed=size, transcendentals=0)


def call_prepare(*args):
    return pl.pallas_call(
        prepare,
        out_shape=(
            struct((NZ * NX, 8, 128), F32), struct((SHARD + 2 * EDGE, CO), BF16), struct((EDGE, C), BF16)
        ),
        in_specs=[ANY, VMEM], out_specs=(VMEM, VMEM, VMEM),
        scratch_shapes=[pltpu.VMEM((FR, 2, W, C), BF16), pltpu.SemaphoreType.DMA((FR,))],
        compiler_params=params(60), cost_estimate=cost(2**16, 2**16),
    )(*args)


def call_pack(*args):
    return pl.pallas_call(
        pack, out_shape=struct((SLABS, 112, HALF), BF16), in_specs=[VMEM] * 4, out_specs=VMEM,
        compiler_params=params(), cost_estimate=cost(2**16, 2**16),
    )(*args)


def call_activate(*args):
    return pl.pallas_call(
        activate, out_shape=(struct((3, 4, 6, T, HALF), BF16), struct((4, 4, T, LAST), BF16)),
        in_specs=[SMEM] + [VMEM] * 4, out_specs=(VMEM, VMEM),
        compiler_params=params(), cost_estimate=cost(2**16, 2**16),
    )(*args)


def call_finish(*args):
    return pl.pallas_call(
        finish, out_shape=struct((T, 4 * CO), BF16), in_specs=[VMEM] * 5, out_specs=VMEM, compiler_params=params(),
        cost_estimate=cost(2**22, 2**20),
    )(*args)


def local(latent, gamma, beta, smooth, weights, w_scale, bias, lengths, order):
    core = lax.axis_index("core")
    latent = latent[0]
    weights = weights.reshape(27, GW, CO)

    spread, to_beside, edge = call_prepare(latent, weights)

    def ring(v):
        return shift(v, lambda y, core, z, x: (y, core, z + 1 - 2 * core, x))

    def along(v, *d):
        def step(y, core, z, x):
            return None if d[core] is None else by_space(y, core, (z * NX + x - d[core]) % (NZ * NX))

        return shift(v, step)

    def other_core(v):
        return shift(v, lambda y, core, z, x: (y, 1 - core, z, x))

    beside, second = along(to_beside, 1, -1), along(weights, None, 2)
    gathered = lax.all_to_all(spread, ("z", "x"), 0, 0, tiled=True)
    edge = along(edge, -1, 1)
    near = beside[:SHARD].reshape(27, GW, CO)
    a0 = jnp.where(core == 0, jnp.stack([weights, near]), jnp.stack([second, near]))
    a1 = ring(a0)
    b1 = shift(a0, lambda y, core, z, x: (y, 1 - core, z - 1 + 2 * core, x))
    windows = call_pack(latent, beside, edge, gathered)
    columns = lax.all_to_all(windows, ("y", "core"), 0, 0, tiled=True)
    a2, b2 = ring(lax.optimization_barrier((a1, b1))[0]), ring(b1)
    a3, b3 = ring(a2), ring(b2)
    act, last = call_activate(lengths, gamma[None], beta[None], smooth[None], columns)
    a4 = ring(a3)


    def part(kernel, *args):
        return pl.pallas_call(
            kernel, out_shape=struct((2, 2, T, CO), F32), in_specs=[VMEM] * len(args), out_specs=VMEM,
            compiler_params=params(32), cost_estimate=cost(2**16, 2**16),
        )(*args)

    pieces = (a0, a1, b1, a2, b2, a3, b3)
    sent = part(functools.partial(convolve, False), act, *pieces)
    other = other_core(part(complete, last, a4, sent))
    keep = part(functools.partial(convolve, True), act, *pieces, a4)
    out = call_finish(order[None], w_scale[None], bias[None], keep, other)
    return out.reshape(SLABS, FR, 2, 2, CO)


def solution(mesh):
    inner = Mesh(mesh.devices.reshape(NY, NC, NZ, NX), AXES)
    slab, space = ("y", "core"), ("z", "x")
    in_specs = (
        P(slab, None, space, None, None), P(), P(), P(), P(None, None, None, space, None), P(), P(), P(), P(),
    )
    out_specs = P(None, None, space, slab, None)
    return jax.shard_map(local, mesh=inner, in_specs=in_specs, out_specs=out_specs, check_vma=False)
```

```python
import functools
import jax
import jax.numpy as jnp
from jax import lax
from jax.experimental import pallas as pl
from jax.experimental.pallas import tpu as pltpu
from jax.sharding import Mesh, PartitionSpec as P

C = 512
CO = 256
GROUPS = 32
GW = C // GROUPS
FR = 4
W = 32
SLABS = 16
T = FR * SLABS
HALF = C // 2
LAST = 384
SHARD = 27 * GW
EDGE = FR * W
NY, NC, NZ, NX = 8, 2, 8, 4
AXES = ("y", "core", "z", "x")
HIGH = lax.Precision.HIGHEST
F32 = jnp.float32
BF16 = jnp.bfloat16
CELLS = 64 * GW
FRAME_CELLS = CELLS * NZ * NX
VMEM = pl.BlockSpec(memory_space=pltpu.VMEM)
SMEM = pl.BlockSpec(memory_space=pltpu.SMEM)
ANY = pl.BlockSpec(memory_space=pl.ANY)


def iota(shape, dim):
    return lax.broadcasted_iota(jnp.int32, shape, dim)


def group_of(shape, channel_dim, group_dim):
    return flag((iota(shape, channel_dim) >> 4) == iota(shape, group_dim))


def flag(condition):
    return condition.astype(F32).astype(BF16)


def bdot(a, b):
    return jnp.dot(a, b, preferred_element_type=F32)


def in_three(v):
    high = v.astype(BF16)
    rest = v - high.astype(F32)
    middle = rest.astype(BF16)
    return high, middle, (rest - middle.astype(F32)).astype(BF16)


def take(v, picks):
    n = v.shape[0]
    pad = -n % 8
    parts = [jnp.concatenate([p.astype(F32), jnp.zeros((pad, v.shape[1]), F32)], axis=0) for p in in_three(v)]
    out = bdot(jnp.concatenate(parts, axis=0).astype(BF16), picks)
    return out[:n] + out[n + pad : 2 * n + pad] + out[2 * (n + pad) : 3 * n + 2 * pad]


def prepare(x_hbm, w_ref, sums_ref, beside_ref, edge_ref, x_ref, sem):
    loads = [pltpu.make_async_copy(x_hbm.at[f], x_ref.at[f], sem.at[f]) for f in range(FR)]
    for copy in loads:
        copy.start()
    beside_ref[:SHARD] = w_ref[...].reshape(SHARD, CO)
    to_groups, to_channels = group_of((C, 128), 0, 1), group_of((128, C), 1, 0)
    rows = []
    for f in range(FR):
        loads[f].wait()
        rows.append(x_ref[f].reshape(2 * W, C).astype(F32))
    totals = jnp.concatenate([jnp.sum(v, axis=0, keepdims=True) for v in rows], axis=0)
    mean = take(totals, to_groups) * (1.0 / CELLS)
    spread = take(mean, to_channels)
    squares = []
    for f in range(FR):
        d = rows[f] - spread[f : f + 1]
        squares.append(jnp.sum(d * d, axis=0, keepdims=True))
    squares = take(jnp.concatenate(squares, axis=0), to_groups)
    core = lax.axis_index("core")
    edge = x_ref[:, core].reshape(EDGE, C)
    beside_ref[SHARD : SHARD + EDGE] = edge[:, :HALF]
    beside_ref[SHARD + EDGE :] = edge[:, HALF:]
    edge_ref[...] = x_ref[:, 1 - core].reshape(EDGE, C)
    sums_ref[...] = jnp.broadcast_to(jnp.concatenate([mean, squares], axis=0)[None], sums_ref.shape)


def join_space(v):
    n = NZ * NX
    mean = jnp.sum(v[:, :FR], axis=0) * (1.0 / n)
    d = v[:, :FR] - mean[None]
    squares = jnp.sum(v[:, FR:], axis=0) + CELLS * jnp.sum(d * d, axis=0)
    return jnp.concatenate([mean, squares], axis=0)


def channel_at(s, core, place):
    step = (place + 2 * GW) >> 6
    nth = jnp.where(step == 0, place >> 4, ((place >> 4) + 2) & 3)
    nth = (nth + 2 * core) & 3
    away = jnp.where(nth == 3, -1, nth)
    away = away + NX * jnp.where(core == 0, -step, step)
    return (((s + away) & (NZ * NX - 1)) << 4) + (place & 15)


def pack(own_ref, beside_ref, edge_ref, sums_ref, out_ref):
    core, s = lax.axis_index("core"), lax.axis_index("z") * NX + lax.axis_index("x")
    beside = jnp.concatenate([beside_ref[SHARD : SHARD + EDGE], beside_ref[SHARD + EDGE :]], axis=1)
    edge, first = edge_ref[...], core == 0
    up, down = jnp.where(first, edge, beside), jnp.where(first, beside, edge)
    source = jnp.concatenate([up, own_ref[...].reshape(2 * EDGE, C), down], axis=0)
    n = 4 * FR * W
    to = iota((n, 1), 0)
    col, row, frame = to >> 4, (to >> 2) & 3, to & 3
    want = jnp.where(
        row == 0,
        frame * W + col,
        jnp.where(row == 3, 3 * EDGE + frame * W + col, EDGE + (frame * 2 + row - 1) * W + col),
    )
    order = flag(want == iota((n, n), 1))
    place = iota((1, C), 1)
    roll = flag(iota((C, C), 0) == channel_at(s, place >> 8, place & (HALF - 1)))
    sorted_rows = bdot(order, source).astype(BF16)
    rolled = bdot(sorted_rows, roll).astype(BF16)
    sums = jnp.concatenate([join_space(sums_ref[...]), jnp.zeros((8, 128), F32)], axis=0)
    thirds = [p[:, :GROUPS] for p in in_three(sums)]
    thirds = jnp.concatenate(thirds + [jnp.zeros((16, HALF - 3 * GROUPS), BF16)], axis=1)
    for y in range(NY):
        for core in range(NC):
            lanes = slice(HALF * core, HALF * (core + 1))
            lo, hi = max(4 * y - 1, 0), min(4 * y + 5, W)
            first = lo - (4 * y - 1)
            out_ref[2 * y + core, 16 * first : 16 * (first + hi - lo), :] = rolled[16 * lo : 16 * hi, lanes]
            out_ref[2 * y + core, 96:112, :] = thirds
            if y == 0:
                out_ref[2 * y + core, 0:16, :] = jnp.zeros((16, HALF), BF16)
            if y == NY - 1:
                out_ref[2 * y + core, 80:96, :] = jnp.zeros((16, HALF), BF16)


def starts(lengths_ref, frame):
    end = lengths_ref[0]
    start = jnp.zeros_like(frame)
    for k in range(1, lengths_ref.shape[0]):
        start = jnp.where(frame >= end, end, start)
        end = end + lengths_ref[k]
    return start


def tables(lengths_ref, gamma_ref, beta_ref, smooth_ref, rows_ref, earlier_ref, means_ref, squares_ref, pick_ref, group_ref, affine_ref):
    core, s = lax.axis_index("core"), lax.axis_index("z") * NX + lax.axis_index("x")
    n = 2 * T
    rows, columns = iota((n, 1), 0), iota((1, n), 1)
    frame_a, frame_b = (rows >> 3) * FR + (rows & 3), (columns >> 3) * FR + (columns & 3)
    same = starts(lengths_ref, frame_a) == starts(lengths_ref, frame_b)
    means_b = (columns & 4) == 0
    means_ref[...] = flag(same & means_b)
    squares_ref[...] = flag(same & jnp.logical_not(means_b))
    pick_ref[...] = flag((frame_b == iota((T, 1), 0)) & means_b)
    channels = channel_at(s, core, iota((1, HALF), 1))
    mine = flag(iota((C, HALF), 0) == channels)
    third = iota((128, 1), 0)
    group_ref[...] = flag(((third & (GROUPS - 1)) == (channels >> 4)) & (third < 3 * GROUPS))
    affine = take(jnp.concatenate([gamma_ref[...], beta_ref[...], smooth_ref[...]], axis=0), mine)
    affine_ref[...] = jnp.concatenate([affine[:2], 1.0 / affine[2:3], jnp.zeros((5, HALF), F32)], axis=0)
    m = 16 * 16
    to = iota((m, 1), 0)
    row, t = to >> 6, to & (T - 1)
    rows_ref[...] = flag(iota((m, m), 1) == (t >> 2) * 16 + row * FR + (t & 3))
    frame, other = iota((T, 1), 0), iota((T, T), 1)
    start = starts(lengths_ref, frame)
    earlier = [flag(other == jnp.maximum(frame - back, start)) for back in (2, 1)]
    earlier_ref[...] = jnp.concatenate(earlier, axis=0)


def activate(rows_ref, earlier_ref, means_ref, squares_ref, pick_ref, group_ref, affine_ref, x_ref, act_ref, last_ref):
    y, s = lax.axis_index("y"), lax.axis_index("z") * NX + lax.axis_index("x")
    n = 2 * T
    thirds = x_ref[:, 96:112, :].astype(F32)[:, :8, :128].reshape(n, 128)
    on_means, on_squares, pick, to_group = means_ref[...], squares_ref[...], pick_ref[...], group_ref[...]
    count = jnp.sum(on_means.astype(F32), axis=1, keepdims=True)

    def whole(v):
        return v[:, :GROUPS] + v[:, GROUPS : 2 * GROUPS] + v[:, 2 * GROUPS : 3 * GROUPS]

    def parts(v):
        return jnp.concatenate(list(in_three(v)) + [jnp.zeros((n, 128 - 3 * GROUPS), BF16)], axis=1)

    mean = whole(bdot(on_means, thirds.astype(BF16))) / count
    off = whole(thirds) - mean
    squares = whole(bdot(on_squares, thirds.astype(BF16))) + FRAME_CELLS * whole(bdot(on_means, parts(off * off)))
    inverse = lax.rsqrt(squares / (count * FRAME_CELLS) + 1e-6)
    gamma, beta, unsmooth = affine_ref[0:1], affine_ref[1:2], affine_ref[2:3]
    mean = bdot(bdot(pick, parts(mean)).astype(BF16), to_group)
    scale = bdot(bdot(pick, parts(inverse)).astype(BF16), to_group) * gamma

    m = 16 * 16
    by_row, earlier = rows_ref[...], earlier_ref[...]
    for c in range(6):
        rows = x_ref[:, 16 * c : 16 * (c + 1), :].reshape(m, HALF)
        values = bdot(by_row, rows)
        for r in range(4):
            v = (values[T * r : T * (r + 1)] - mean) * scale + beta
            v = v / (1.0 + jnp.exp(-v)) * unsmooth
            inside = None
            if r == 0:
                inside = s > 0
            if r == 3:
                inside = s < NZ * NX - 1
            if c == 0:
                inside = (y > 0) if inside is None else inside & (y > 0)
            if c == 5:
                inside = (y < NY - 1) if inside is None else inside & (y < NY - 1)
            if inside is not None:
                v = v * inside.astype(F32)
            v = v.astype(BF16)
            act_ref[2, r, c] = v
            e = bdot(earlier, v).astype(BF16)
            act_ref[0, r, c] = e[:T]
            act_ref[1, r, c] = e[T:]
    for r in range(4):
        for c in range(4):
            taps = [act_ref[j, r, c + b, :, HALF - 2 * GW :] for j in range(3) for b in range(3)]
            last_ref[r, c] = jnp.concatenate(taps + [jnp.zeros((T, LAST - 18 * GW), BF16)], axis=1)


def convolve(own_columns, act_ref, *refs):
    weights, out_ref = refs[:-1], refs[-1]
    core = lax.axis_index("core")
    column = 2 * core if own_columns else 2 - 2 * core
    total = None
    for tap in range(27):
        j, a, b = tap // 9, tap // 3 % 3, tap % 3
        lhs = act_ref[j, a : a + 2, pl.ds(column + b, 2)].reshape(4 * T, HALF)
        rows = jnp.concatenate([v[i, tap] for v in weights for i in range(2)], axis=0)
        term = bdot(lhs[:, : rows.shape[0]], rows)
        total = term if total is None else total + term
    out_ref[...] = total.reshape(2, 2, T, CO)


def complete(last_ref, w_ref, part_ref, out_ref):
    column = 2 - 2 * lax.axis_index("core")
    total = part_ref[...].reshape(4 * T, CO)
    for a in range(3):
        lhs = last_ref[a : a + 2, pl.ds(column, 2)].reshape(4 * T, LAST)
        rows = [w_ref[i, 9 * j + 3 * a + b] for j in range(3) for b in range(3) for i in range(2)]
        total = total + bdot(lhs, jnp.concatenate(rows + [jnp.zeros((LAST - 18 * GW, CO), BF16)], axis=0))
    out_ref[...] = total.reshape(2, 2, T, CO)


def finish(order_ref, scale_ref, bias_ref, a_ref, b_ref, out_ref):
    picked = (iota((T, T), 0) == order_ref[...]).astype(F32).astype(BF16)
    for r in range(2):
        for c in range(2):
            v = ((a_ref[r, c] + b_ref[r, c]) * scale_ref[...] + bias_ref[...]).astype(BF16)
            v = lax.dot_general(picked, v, (((0,), (0,)), ((), ())), preferred_element_type=F32)
            at = (2 * r + c) * CO
            out_ref[:, at : at + CO] = v.astype(BF16)


def shift(value, step):
    pairs = []
    for i in range(NY * NC * NZ * NX):
        y, core, z, x = i // 64, i // 32 % 2, i // 4 % 8, i % 4
        to = step(y, core, z, x)
        if to is not None:
            ty, tc, tz, tx = to
            pairs.append((i, ((ty * NC + tc) * NZ + tz % NZ) * NX + tx))
    return lax.ppermute(value, AXES, pairs)


def by_space(y, core, s):
    return (y, core, s // NX, s % NX) if 0 <= s < NZ * NX else None


def struct(shape, dtype):
    return jax.ShapeDtypeStruct(shape, dtype)


def params(mib=48):
    return pltpu.CompilerParams(vmem_limit_bytes=mib * 2**20)


def cost(flops, size):
    return pl.CostEstimate(flops=flops, bytes_accessed=size, transcendentals=0)


def call_prepare(*args):
    return pl.pallas_call(
        prepare,
        out_shape=(
            struct((NZ * NX, 8, 128), F32), struct((SHARD + 2 * EDGE, CO), BF16), struct((EDGE, C), BF16)
        ),
        in_specs=[ANY, VMEM], out_specs=(VMEM, VMEM, VMEM),
        scratch_shapes=[pltpu.VMEM((FR, 2, W, C), BF16), pltpu.SemaphoreType.DMA((FR,))],
        compiler_params=params(60), cost_estimate=cost(2**16, 2**16),
    )(*args)


def call_pack(*args):
    return pl.pallas_call(
        pack, out_shape=struct((SLABS, 112, HALF), BF16), in_specs=[VMEM] * 4, out_specs=VMEM,
        compiler_params=params(), cost_estimate=cost(2**16, 2**16),
    )(*args)


def call_tables(*args):
    shapes = (2 * HALF // 2, HALF), (2 * T, T), (2 * T, 2 * T), (2 * T, 2 * T), (T, 2 * T), (128, HALF)
    return pl.pallas_call(
        tables, out_shape=tuple(struct(shape, BF16) for shape in shapes) + (struct((8, HALF), F32),),
        in_specs=[SMEM] + [VMEM] * 3, out_specs=(VMEM,) * 7, compiler_params=params(16),
        cost_estimate=cost(2**16, 2**16),
    )(*args)


def call_activate(*args):
    return pl.pallas_call(
        activate, out_shape=(struct((3, 4, 6, T, HALF), BF16), struct((4, 4, T, LAST), BF16)),
        in_specs=[VMEM] * 8, out_specs=(VMEM, VMEM),
        compiler_params=params(), cost_estimate=cost(2**16, 2**16),
    )(*args)


def call_finish(*args):
    return pl.pallas_call(
        finish, out_shape=struct((T, 4 * CO), BF16), in_specs=[VMEM] * 5, out_specs=VMEM, compiler_params=params(),
        cost_estimate=cost(2**22, 2**20),
    )(*args)


def local(latent, gamma, beta, smooth, weights, w_scale, bias, lengths, order):
    core = lax.axis_index("core")
    latent = latent[0]
    weights = weights.reshape(27, GW, CO)

    spread, to_beside, edge = call_prepare(latent, weights)

    def ring(v):
        return shift(v, lambda y, core, z, x: (y, core, z + 1 - 2 * core, x))

    def along(v, *d):
        def step(y, core, z, x):
            return None if d[core] is None else by_space(y, core, (z * NX + x - d[core]) % (NZ * NX))

        return shift(v, step)

    def other_core(v):
        return shift(v, lambda y, core, z, x: (y, 1 - core, z, x))

    beside, second = along(to_beside, 1, -1), along(weights, None, 2)
    gathered = lax.all_to_all(spread, ("z", "x"), 0, 0, tiled=True)
    edge = along(edge, -1, 1)
    near = beside[:SHARD].reshape(27, GW, CO)
    a0 = jnp.where(core == 0, jnp.stack([weights, near]), jnp.stack([second, near]))
    a1 = ring(a0)
    b1 = shift(a0, lambda y, core, z, x: (y, 1 - core, z - 1 + 2 * core, x))
    windows = call_pack(latent, beside, edge, gathered)
    columns = lax.all_to_all(windows, ("y", "core"), 0, 0, tiled=True)
    a2, b2 = ring(lax.optimization_barrier((a1, b1))[0]), ring(b1)
    known = call_tables(lengths, gamma[None], beta[None], smooth[None])
    a2, known = lax.optimization_barrier((a2, known))
    a3, b3 = ring(a2), ring(b2)
    act, last = call_activate(*known, columns)
    a4 = ring(a3)


    def part(kernel, *args):
        return pl.pallas_call(
            kernel, out_shape=struct((2, 2, T, CO), F32), in_specs=[VMEM] * len(args), out_specs=VMEM,
            compiler_params=params(32), cost_estimate=cost(2**16, 2**16),
        )(*args)

    pieces = (a0, a1, b1, a2, b2, a3, b3)
    sent = part(functools.partial(convolve, False), act, *pieces)
    other = other_core(part(complete, last, a4, sent))
    keep = part(functools.partial(convolve, True), act, *pieces, a4)
    out = call_finish(order[None], w_scale[None], bias[None], keep, other)
    return out.reshape(SLABS, FR, 2, 2, CO)


def solution(mesh):
    inner = Mesh(mesh.devices.reshape(NY, NC, NZ, NX), AXES)
    slab, space = ("y", "core"), ("z", "x")
    in_specs = (
        P(slab, None, space, None, None), P(), P(), P(), P(None, None, None, space, None), P(), P(), P(), P(),
    )
    out_specs = P(None, None, space, slab, None)
    return jax.shard_map(local, mesh=inner, in_specs=in_specs, out_specs=out_specs, check_vma=False)
```

```python
import functools
import jax
import jax.numpy as jnp
from jax import lax
from jax.experimental import pallas as pl
from jax.experimental.pallas import tpu as pltpu
from jax.sharding import Mesh, PartitionSpec as P

C = 512
CO = 256
GROUPS = 32
GW = C // GROUPS
FR = 4
W = 32
SLABS = 16
T = FR * SLABS
HALF = C // 2
LAST = 384
SHARD = 27 * GW
EDGE = FR * W
NY, NC, NZ, NX = 8, 2, 8, 4
AXES = ("y", "core", "z", "x")
HIGH = lax.Precision.HIGHEST
F32 = jnp.float32
BF16 = jnp.bfloat16
CELLS = 64 * GW
FRAME_CELLS = CELLS * NZ * NX
VMEM = pl.BlockSpec(memory_space=pltpu.VMEM)
SMEM = pl.BlockSpec(memory_space=pltpu.SMEM)
ANY = pl.BlockSpec(memory_space=pl.ANY)


def iota(shape, dim):
    return lax.broadcasted_iota(jnp.int32, shape, dim)


def group_of(shape, channel_dim, group_dim):
    return flag((iota(shape, channel_dim) >> 4) == iota(shape, group_dim))


def flag(condition):
    return condition.astype(F32).astype(BF16)


def bdot(a, b):
    return jnp.dot(a, b, preferred_element_type=F32)


def in_three(v):
    high = v.astype(BF16)
    rest = v - high.astype(F32)
    middle = rest.astype(BF16)
    return high, middle, (rest - middle.astype(F32)).astype(BF16)


def take(v, picks):
    n = v.shape[0]
    pad = -n % 8
    parts = [jnp.concatenate([p.astype(F32), jnp.zeros((pad, v.shape[1]), F32)], axis=0) for p in in_three(v)]
    out = bdot(jnp.concatenate(parts, axis=0).astype(BF16), picks)
    return out[:n] + out[n + pad : 2 * n + pad] + out[2 * (n + pad) : 3 * n + 2 * pad]


def prepare(x_hbm, w_ref, sums_ref, beside_ref, edge_ref, x_ref, sem):
    loads = [pltpu.make_async_copy(x_hbm.at[f], x_ref.at[f], sem.at[f]) for f in range(FR)]
    for copy in loads:
        copy.start()
    beside_ref[:SHARD] = w_ref[...].reshape(SHARD, CO)
    to_groups, to_channels = group_of((C, 128), 0, 1), group_of((128, C), 1, 0)
    rows = []
    for f in range(FR):
        loads[f].wait()
        rows.append(x_ref[f].reshape(2 * W, C).astype(F32))
    totals = jnp.concatenate([jnp.sum(v, axis=0, keepdims=True) for v in rows], axis=0)
    mean = take(totals, to_groups) * (1.0 / CELLS)
    spread = take(mean, to_channels)
    squares = []
    for f in range(FR):
        d = rows[f] - spread[f : f + 1]
        squares.append(jnp.sum(d * d, axis=0, keepdims=True))
    squares = take(jnp.concatenate(squares, axis=0), to_groups)
    core = lax.axis_index("core")
    edge = x_ref[:, core].reshape(EDGE, C)
    beside_ref[SHARD : SHARD + EDGE] = edge[:, :HALF]
    beside_ref[SHARD + EDGE :] = edge[:, HALF:]
    edge_ref[...] = x_ref[:, 1 - core].reshape(EDGE, C)
    sums_ref[...] = jnp.broadcast_to(jnp.concatenate([mean, squares], axis=0)[None], sums_ref.shape)


def join_space(v):
    n = NZ * NX
    mean = jnp.sum(v[:, :FR], axis=0) * (1.0 / n)
    d = v[:, :FR] - mean[None]
    squares = jnp.sum(v[:, FR:], axis=0) + CELLS * jnp.sum(d * d, axis=0)
    return jnp.concatenate([mean, squares], axis=0)


def channel_at(s, core, place):
    step = (place + 2 * GW) >> 6
    nth = jnp.where(step == 0, place >> 4, ((place >> 4) + 2) & 3)
    nth = (nth + 2 * core) & 3
    away = jnp.where(nth == 3, -1, nth)
    away = away + NX * jnp.where(core == 0, -step, step)
    return (((s + away) & (NZ * NX - 1)) << 4) + (place & 15)


def pack(own_ref, beside_ref, edge_ref, sums_ref, out_ref):
    core, s = lax.axis_index("core"), lax.axis_index("z") * NX + lax.axis_index("x")
    beside = jnp.concatenate([beside_ref[SHARD : SHARD + EDGE], beside_ref[SHARD + EDGE :]], axis=1)
    edge, first = edge_ref[...], core == 0
    up, down = jnp.where(first, edge, beside), jnp.where(first, beside, edge)
    source = jnp.concatenate([up, own_ref[...].reshape(2 * EDGE, C), down], axis=0)
    n = 4 * FR * W
    to = iota((n, 1), 0)
    col, row, frame = to >> 4, (to >> 2) & 3, to & 3
    want = jnp.where(
        row == 0,
        frame * W + col,
        jnp.where(row == 3, 3 * EDGE + frame * W + col, EDGE + (frame * 2 + row - 1) * W + col),
    )
    order = flag(want == iota((n, n), 1))
    place = iota((1, C), 1)
    roll = flag(iota((C, C), 0) == channel_at(s, place >> 8, place & (HALF - 1)))
    sorted_rows = bdot(order, source).astype(BF16)
    rolled = bdot(sorted_rows, roll).astype(BF16)
    sums = jnp.concatenate([join_space(sums_ref[...]), jnp.zeros((8, 128), F32)], axis=0)
    thirds = [p[:, :GROUPS] for p in in_three(sums)]
    thirds = jnp.concatenate(thirds + [jnp.zeros((16, HALF - 3 * GROUPS), BF16)], axis=1)
    for y in range(NY):
        for core in range(NC):
            lanes = slice(HALF * core, HALF * (core + 1))
            lo, hi = max(4 * y - 1, 0), min(4 * y + 5, W)
            first = lo - (4 * y - 1)
            out_ref[2 * y + core, 16 * first : 16 * (first + hi - lo), :] = rolled[16 * lo : 16 * hi, lanes]
            out_ref[2 * y + core, 96:112, :] = thirds
            if y == 0:
                out_ref[2 * y + core, 0:16, :] = jnp.zeros((16, HALF), BF16)
            if y == NY - 1:
                out_ref[2 * y + core, 80:96, :] = jnp.zeros((16, HALF), BF16)


def starts(lengths_ref, frame):
    end = lengths_ref[0]
    start = jnp.zeros_like(frame)
    for k in range(1, lengths_ref.shape[0]):
        start = jnp.where(frame >= end, end, start)
        end = end + lengths_ref[k]
    return start


def activate(lengths_ref, gamma_ref, beta_ref, smooth_ref, x_ref, act_ref, last_ref):
    y, core, s = lax.axis_index("y"), lax.axis_index("core"), lax.axis_index("z") * NX + lax.axis_index("x")
    n = 2 * T
    thirds = x_ref[:, 96:112, :].astype(F32)[:, :8, :128].reshape(n, 128)
    rows, columns = iota((n, 1), 0), iota((1, n), 1)
    frame_a, frame_b = (rows >> 3) * FR + (rows & 3), (columns >> 3) * FR + (columns & 3)
    same = starts(lengths_ref, frame_a) == starts(lengths_ref, frame_b)
    means_b = (columns & 4) == 0
    on_means, on_squares = same & means_b, flag(same & jnp.logical_not(means_b))
    count = jnp.sum(on_means.astype(F32), axis=1, keepdims=True)
    on_means = flag(on_means)

    def whole(v):
        return v[:, :GROUPS] + v[:, GROUPS : 2 * GROUPS] + v[:, 2 * GROUPS : 3 * GROUPS]

    def parts(v):
        return jnp.concatenate(list(in_three(v)) + [jnp.zeros((n, 128 - 3 * GROUPS), BF16)], axis=1)

    mean = whole(bdot(on_means, thirds.astype(BF16))) / count
    off = whole(thirds) - mean
    squares = whole(bdot(on_squares, thirds.astype(BF16))) + FRAME_CELLS * whole(bdot(on_means, parts(off * off)))
    inverse = lax.rsqrt(squares / (count * FRAME_CELLS) + 1e-6)
    pick = flag((frame_b == iota((T, 1), 0)) & means_b)
    channels = channel_at(s, core, iota((1, HALF), 1))
    mine = flag(iota((C, HALF), 0) == channels)
    third = iota((128, 1), 0)
    to_group = flag(((third & (GROUPS - 1)) == (channels >> 4)) & (third < 3 * GROUPS))
    affine = take(jnp.concatenate([gamma_ref[...], beta_ref[...], smooth_ref[...]], axis=0), mine)
    gamma, beta, unsmooth = affine[0:1], affine[1:2], 1.0 / affine[2:3]
    mean = bdot(bdot(pick, parts(mean)).astype(BF16), to_group)
    scale = bdot(bdot(pick, parts(inverse)).astype(BF16), to_group) * gamma

    m = 16 * 16
    to = iota((m, 1), 0)
    row, t = to >> 6, to & (T - 1)
    by_row = flag(iota((m, m), 1) == (t >> 2) * 16 + row * FR + (t & 3))
    frame, other = iota((T, 1), 0), iota((T, T), 1)
    start = starts(lengths_ref, frame)
    earlier = [flag(other == jnp.maximum(frame - back, start)) for back in (2, 1)]
    earlier = jnp.concatenate(earlier, axis=0)
    for c in range(6):
        rows = x_ref[:, 16 * c : 16 * (c + 1), :].reshape(m, HALF)
        values = bdot(by_row, rows)
        for r in range(4):
            v = (values[T * r : T * (r + 1)] - mean) * scale + beta
            v = v / (1.0 + jnp.exp(-v)) * unsmooth
            inside = None
            if r == 0:
                inside = s > 0
            if r == 3:
                inside = s < NZ * NX - 1
            if c == 0:
                inside = (y > 0) if inside is None else inside & (y > 0)
            if c == 5:
                inside = (y < NY - 1) if inside is None else inside & (y < NY - 1)
            if inside is not None:
                v = v * inside.astype(F32)
            v = v.astype(BF16)
            act_ref[2, r, c] = v
            e = bdot(earlier, v).astype(BF16)
            act_ref[0, r, c] = e[:T]
            act_ref[1, r, c] = e[T:]
    for r in range(4):
        for c in range(4):
            taps = [act_ref[j, r, c + b, :, HALF - 2 * GW :] for j in range(3) for b in range(3)]
            last_ref[r, c] = jnp.concatenate(taps + [jnp.zeros((T, LAST - 18 * GW), BF16)], axis=1)


def convolve(own_columns, act_ref, *refs):
    weights, out_ref = refs[:-1], refs[-1]
    core = lax.axis_index("core")
    column = 2 * core if own_columns else 2 - 2 * core
    total = None
    for tap in range(27):
        j, a, b = tap // 9, tap // 3 % 3, tap % 3
        lhs = act_ref[j, a : a + 2, pl.ds(column + b, 2)].reshape(4 * T, HALF)
        rows = jnp.concatenate([v[i, tap] for v in weights for i in range(2)], axis=0)
        term = bdot(lhs[:, : rows.shape[0]], rows)
        total = term if total is None else total + term
    out_ref[...] = total.reshape(2, 2, T, CO)


def complete(last_ref, w_ref, part_ref, out_ref):
    column = 2 - 2 * lax.axis_index("core")
    total = part_ref[...].reshape(4 * T, CO)
    for a in range(3):
        lhs = last_ref[a : a + 2, pl.ds(column, 2)].reshape(4 * T, LAST)
        rows = [w_ref[i, 9 * j + 3 * a + b] for j in range(3) for b in range(3) for i in range(2)]
        total = total + bdot(lhs, jnp.concatenate(rows + [jnp.zeros((LAST - 18 * GW, CO), BF16)], axis=0))
    out_ref[...] = total.reshape(2, 2, T, CO)


def finish(order_ref, scale_ref, bias_ref, a_ref, b_ref, out_ref):
    picked = (iota((T, T), 0) == order_ref[...]).astype(F32).astype(BF16)
    for r in range(2):
        for c in range(2):
            v = ((a_ref[r, c] + b_ref[r, c]) * scale_ref[...] + bias_ref[...]).astype(BF16)
            v = lax.dot_general(picked, v, (((0,), (0,)), ((), ())), preferred_element_type=F32)
            at = (2 * r + c) * CO
            out_ref[:, at : at + CO] = v.astype(BF16)


def shift(value, step):
    pairs = []
    for i in range(NY * NC * NZ * NX):
        y, core, z, x = i // 64, i // 32 % 2, i // 4 % 8, i % 4
        to = step(y, core, z, x)
        if to is not None:
            ty, tc, tz, tx = to
            pairs.append((i, ((ty * NC + tc) * NZ + tz % NZ) * NX + tx))
    return lax.ppermute(value, AXES, pairs)


def by_space(y, core, s):
    return (y, core, s // NX, s % NX) if 0 <= s < NZ * NX else None


def struct(shape, dtype):
    return jax.ShapeDtypeStruct(shape, dtype)


def params(mib=48):
    return pltpu.CompilerParams(vmem_limit_bytes=mib * 2**20)


def cost(flops, size):
    return pl.CostEstimate(flops=flops, bytes_accessed=size, transcendentals=0)


def call_prepare(*args):
    return pl.pallas_call(
        prepare,
        out_shape=(
            struct((NZ * NX, 8, 128), F32), struct((SHARD + 2 * EDGE, CO), BF16), struct((EDGE, C), BF16)
        ),
        in_specs=[ANY, VMEM], out_specs=(VMEM, VMEM, VMEM),
        scratch_shapes=[pltpu.VMEM((FR, 2, W, C), BF16), pltpu.SemaphoreType.DMA((FR,))],
        compiler_params=params(60), cost_estimate=cost(2**16, 2**16),
    )(*args)


def call_pack(*args):
    return pl.pallas_call(
        pack, out_shape=struct((SLABS, 112, HALF), BF16), in_specs=[VMEM] * 4, out_specs=VMEM,
        compiler_params=params(), cost_estimate=cost(2**16, 2**16),
    )(*args)


def call_activate(*args):
    return pl.pallas_call(
        activate, out_shape=(struct((3, 4, 6, T, HALF), BF16), struct((4, 4, T, LAST), BF16)),
        in_specs=[SMEM] + [VMEM] * 4, out_specs=(VMEM, VMEM),
        compiler_params=params(), cost_estimate=cost(2**16, 2**16),
    )(*args)


def call_finish(*args):
    return pl.pallas_call(
        finish, out_shape=struct((T, 4 * CO), BF16), in_specs=[VMEM] * 5, out_specs=VMEM, compiler_params=params(),
        cost_estimate=cost(2**22, 2**20),
    )(*args)


def local(latent, gamma, beta, smooth, weights, w_scale, bias, lengths, order):
    core = lax.axis_index("core")
    latent = latent[0]
    weights = weights.reshape(27, GW, CO)

    spread, to_beside, edge = call_prepare(latent, weights)

    def ring(v):
        return shift(v, lambda y, core, z, x: (y, core, z + 1 - 2 * core, x))

    def along(v, *d):
        def step(y, core, z, x):
            return None if d[core] is None else by_space(y, core, (z * NX + x - d[core]) % (NZ * NX))

        return shift(v, step)

    def other_core(v):
        return shift(v, lambda y, core, z, x: (y, 1 - core, z, x))

    beside, second = along(to_beside, 1, -1), along(weights, None, 2)
    gathered = lax.all_to_all(spread, ("z", "x"), 0, 0, tiled=True)
    near = beside[:SHARD].reshape(27, GW, CO)
    a0 = jnp.where(core == 0, jnp.stack([weights, near]), jnp.stack([second, near]))
    edge = along(lax.optimization_barrier((edge, a0))[0], -1, 1)
    a1 = ring(a0)
    b1 = shift(a0, lambda y, core, z, x: (y, 1 - core, z - 1 + 2 * core, x))
    windows = call_pack(latent, beside, edge, gathered)
    columns = lax.all_to_all(windows, ("y", "core"), 0, 0, tiled=True)
    a2, b2 = ring(lax.optimization_barrier((a1, b1))[0]), ring(b1)
    a3, b3 = ring(a2), ring(b2)
    act, last = call_activate(lengths, gamma[None], beta[None], smooth[None], columns)
    a4 = ring(a3)


    def part(kernel, *args):
        return pl.pallas_call(
            kernel, out_shape=struct((2, 2, T, CO), F32), in_specs=[VMEM] * len(args), out_specs=VMEM,
            compiler_params=params(32), cost_estimate=cost(2**16, 2**16),
        )(*args)

    pieces = (a0, a1, b1, a2, b2, a3, b3)
    sent = part(functools.partial(convolve, False), act, *pieces)
    other = other_core(part(complete, last, a4, sent))
    keep = part(functools.partial(convolve, True), act, *pieces, a4)
    out = call_finish(order[None], w_scale[None], bias[None], keep, other)
    return out.reshape(SLABS, FR, 2, 2, CO)


def solution(mesh):
    inner = Mesh(mesh.devices.reshape(NY, NC, NZ, NX), AXES)
    slab, space = ("y", "core"), ("z", "x")
    in_specs = (
        P(slab, None, space, None, None), P(), P(), P(), P(None, None, None, space, None), P(), P(), P(), P(),
    )
    out_specs = P(None, None, space, slab, None)
    return jax.shard_map(local, mesh=inner, in_specs=in_specs, out_specs=out_specs, check_vma=False)
```
